256 devices in a mesh: axial: 16 (over x, y), pitch: 16 (over z, core).
Axes of the slice: x: 4, y: 4, z: 8, core: 2. Of those that a mesh axis runs over, the one named last changes fastest.
Arguments:
- adjoint_start: float32 [128, 35, 2048], P('axial', None, 'pitch'), may hold values from -6 to 6
- source: float32 [128, 35, 2048], P('axial', None, 'pitch'), may hold values from -0.07 to 0.07
- couple_block: float32 [128, 35, 35], P('axial'), may hold values from -0.05 to 2.9, as said below
- shift_diag: float32 [128, 35], P('axial'), may hold values from 0.0005 to 0.0015
- pitch_gain: float32 [128, 35], P('axial'), may hold values from 0.0003 to 0.001
- row_map: int32 [2048], replicated, may hold values from 0 to 2047, each once
- slide: int32 [7], replicated, may hold values from 0 to 2047
Outputs:
- adjoint_field: float32 [128, 35, 2048], P('axial', None, 'pitch')
The draws below stay inside these ranges and needn't reach their ends.
Inputs may be any that keep to these rules, and one draw needn't show every extreme that they name: `row_map`: each line number appears once. `couple_block`: symmetric in its last two dimensions; each diagonal entry exceeds the sum of the magnitudes of the other entries of its row by 0.3 or more.
All inputs are finite; a program needn't handle non-finite values.
Results may differ from the reference program's by a relative error of at most 0.0003.
Values sent between devices are 32-bit elements; how exact they have to be, the bound alone decides.
A program may use at most 64 MiB of HBM per device.

```python
import math
import jax
import jax.numpy as jnp
from jax import lax

INST = 7
VARS = 5
B = 35
SWEEPS = 2
NA = 128
NL = 2048


def draw_source(key, part):
    key = jax.random.fold_in(key, 11)
    return 0.02 * jax.random.truncated_normal(key, -3.5, 3.5, (NA, B, NL), jnp.float32)


def draw_couple_block(key, part):
    key = jax.random.fold_in(key, 5)
    first, second = jax.random.split(key)
    spread = 0.05
    raw = jax.random.uniform(first, (NA, B, B), jnp.float32, -spread, spread)
    mixed = 0.5 * (raw + jnp.swapaxes(raw, 1, 2))
    leading = 34.0 * spread + jax.random.uniform(second, (NA, B, 1), jnp.float32, 0.3, 1.2)
    diagonal = jnp.arange(B)[:, None] == jnp.arange(B)[None, :]
    return jnp.where(diagonal[None], leading, mixed)


def place_ends(result, key, smallest, largest):
    index_at = [jax.random.randint(jax.random.fold_in(key, axis), (), 0, length) for axis, length in enumerate(result.shape)]
    longest = result.shape.index(max(result.shape))
    beside = index_at[:longest] + [(index_at[longest] + 1) % result.shape[longest]] + index_at[longest + 1:]
    return result.at[tuple(index_at)].set(smallest).at[tuple(beside)].set(largest)


def level_of(key, shape, cuts, least, top_value):
    level, own = 1.0, jax.random.fold_in(key, 6)
    for axis_at, blocks in cuts:
        heights = jnp.exp(jax.random.uniform(jax.random.fold_in(own, axis_at), (blocks,), jnp.float32, least / len(cuts), top_value / len(cuts)))
        level = level * jnp.repeat(heights, shape[axis_at] // blocks).reshape([-1 if axis == axis_at else 1 for axis in range(len(shape))])
    return level


def scatter_about(rng, extent, deviation, most, cuts=(), held_as=jnp.bfloat16):
    result = jax.random.normal(rng, extent, jnp.float32) * deviation
    if len(cuts) > 0:
        result = level_of(rng, extent, cuts, -0.22, 0.18) * result
    return jnp.clip(result, min=-most, max=most).astype(held_as)


def setup_inputs(seed: int = 0) -> dict:
    key_of = jax.random.split(jax.random.key(seed), 8)
    return {
        "adjoint_start": scatter_about(key_of[0], (NA, B, NL), 1.0, 6.0, ((0, 16), (2, 16)), jnp.float32),
        "source": draw_source(jax.random.fold_in(key_of[7], 71), 0),
        "couple_block": draw_couple_block(jax.random.fold_in(key_of[7], 71), 0),
        "shift_diag": jnp.clip(jnp.exp(math.log(0.0015) - 1.09861225 * jax.random.uniform(key_of[3], (NA, B), jnp.float32) ** level_of(key_of[3], (NA, B), ((0, 16),), -0.2, 0.2)), 0.0005, 0.0015),
        "pitch_gain": jnp.clip(jnp.exp(math.log(0.001) - 1.2039728 * jax.random.uniform(key_of[4], (NA, B), jnp.float32) ** level_of(key_of[4], (NA, B), ((0, 16),), -0.2, 0.2)), 0.0003, 0.001),
        "row_map": jax.random.permutation(key_of[5], NL).astype(jnp.int32),
        "slide": place_ends(jax.random.randint(key_of[6], (INST,), 0, NL), jax.random.fold_in(key_of[6], 1), 0, NL - 1).astype(jnp.int32),
    }


HIGHEST = lax.Precision.HIGHEST

def inverse(matrix):
    factor = jnp.linalg.cholesky(matrix)
    return jax.scipy.linalg.cho_solve((factor, True), jnp.eye(matrix.shape[0], dtype=jnp.float32))

def reference(adjoint_start, source, couple_block, shift_diag, pitch_gain, row_map, slide):
    half = NA // 2
    eye = jnp.eye(B, dtype=jnp.float32)
    before_link = jnp.concatenate([jnp.zeros((1, B, B), jnp.float32), couple_block[:-1]], 0)
    keep = jnp.ones((NA,), jnp.float32).at[half - 1].set(0.0).at[NA - 1].set(0.0)
    link = couple_block * keep[:, None, None]
    diag_full = before_link + couple_block + (shift_diag + 2.0 * pitch_gain)[:, :, None] * eye
    lookup = ((row_map[None, :] + jnp.repeat(slide, VARS)[:, None]) % NL).astype(jnp.int32)

    def factor_step(current, inputs):
        diagonal, coupling = inputs
        inverted = inverse(current)
        forward = jnp.dot(coupling, inverted, precision=HIGHEST)
        return (diagonal - jnp.dot(forward, coupling, precision=HIGHEST), (inverted, forward))
    last_pivot, (inverses, forwards) = lax.scan(factor_step, diag_full[0], (diag_full[1:], link[:-1]))
    inverses = jnp.concatenate([inverses, inverse(last_pivot)[None]], 0)
    backwards = jnp.swapaxes(forwards, 1, 2)

    def down(carry, inputs):
        row, forward = inputs
        return (row + jnp.dot(forward, carry, precision=HIGHEST), carry)

    def up(carry, inputs):
        row, inverted, backward = inputs
        value = jnp.dot(inverted, row, precision=HIGHEST) + jnp.dot(backward, carry, precision=HIGHEST)
        return (value, value)
    field = adjoint_start
    for sweep in range(SWEEPS):
        mapped = jnp.take_along_axis(field[half - 1], lookup, axis=1)
        below = jnp.concatenate([jnp.zeros((1, B, NL), jnp.float32), field[:-1]], 0).at[half].set(mapped)
        above = jnp.concatenate([field[1:], jnp.zeros((1, B, NL), jnp.float32)], 0)
        applied = jnp.einsum('ibc,icj->ibj', diag_full, field, precision=HIGHEST) - jnp.einsum('ibc,icj->ibj', before_link, below, precision=HIGHEST) - jnp.einsum('ibc,icj->ibj', couple_block, above, precision=HIGHEST) - pitch_gain[:, :, None] * (jnp.roll(field, 1, 2) + jnp.roll(field, -1, 2))
        residual = source - applied
        last_row, rows = lax.scan(down, residual[0], (residual[1:], forwards))
        rows = jnp.concatenate([rows, last_row[None]], 0)
        last_value = jnp.dot(inverses[-1], rows[-1], precision=HIGHEST)
        _, values = lax.scan(up, last_value, (rows[:-1], inverses[:-1], backwards), reverse=True)
        update = jnp.concatenate([values, last_value[None]], 0)
        field = field + update
    return field
```

```python
import functools
import math

import jax
import jax.numpy as jnp
import numpy as np
from jax import lax
from jax.experimental import pallas as pl
from jax.experimental.pallas import tpu as pltpu
from jax.sharding import PartitionSpec as P

INST, VARS, B = 7, 5, 35
CELLS, LINES, CHAIN = 8, 128, 8
NI = 256
NR = 288
NF = 384
F32, BF16, I32 = jnp.float32, jnp.bfloat16, jnp.int32
HIGHEST = lax.Precision.HIGHEST
MESH = pl.DeviceIdType.MESH

C_LOW, C_HIGH, G_LOW, G_HIGH = 0.299, 5.51, 0.00109, 0.00352
LOCAL_STEPS, REDUCED_STEPS = 7, 7


def scalar_bounds(stator):
    ends = []
    for c, g in ((C_LOW, G_LOW), (C_HIGH, G_HIGH)):
        n = CELLS * CHAIN
        t = np.diag(np.full(n, 2 * c + g)) - c * np.eye(n, k=1) - c * np.eye(n, k=-1)
        if not stator:
            t[0, 0] -= c
        keep = np.arange(0, n, CELLS)
        rest = np.setdiff1d(np.arange(n), keep)
        s = t[np.ix_(keep, keep)] - t[np.ix_(keep, rest)] @ np.linalg.solve(
            t[np.ix_(rest, rest)], t[np.ix_(rest, keep)]
        )
        ends.append(np.linalg.eigvalsh(s))
    return float(ends[0][0]), float(ends[1][-1])


def local_bounds():
    bend = 2 * math.cos(math.pi / CELLS)
    return C_LOW * (2 - bend) + G_LOW, C_HIGH * (2 + bend) + G_HIGH


def plan(bounds, steps):
    low, high = bounds
    mid, half = 0.5 * (high + low), 0.5 * (high - low)
    t = first = mid / half
    for _ in range(steps):
        t = 2 * t * t - 1
    return mid, half, first, 1.0 / t


def dot(a, b, precision=None, dims=((1,), (0,))):
    return lax.dot_general(a, b, (dims, ((), ())), precision=precision, preferred_element_type=F32)


def split(x):
    high = x.astype(BF16)
    return high, (x - high.astype(F32)).astype(BF16)


def dot3(a, b):
    (ah, al), (bh, bl) = a, b
    return dot(ah, bh) + (dot(ah, bl) + dot(al, bh))


def iota(shape, axis):
    return lax.broadcasted_iota(I32, shape, axis)


def block_of(index, count):
    return sum(((index >= B * k).astype(I32) for k in range(1, count)), jnp.zeros_like(index))


def ones(mask):
    return jnp.where(mask, 1.0, 0.0).astype(F32)


def chebyshev(n, start, first, lhs, rhs, y_ref, t_ref, steps):
    def step(_, t):
        th, tl = split(t_ref[...])
        yh, yl = split(y_ref[...])
        lhs[0:n, 0:n] = th
        lhs[n : 2 * n, 0:n] = yh
        lhs[2 * n : 3 * n, 0:n] = tl
        lhs[3 * n : 4 * n, 0:n] = yl
        rhs[0:n, 0:n] = th
        rhs[n : 2 * n, 0:n] = tl
        big = dot(lhs[0 : 4 * n, 0:n], rhs[0:n, 0:n])
        small = dot(lhs[0 : 2 * n, 0:n], rhs[n : 2 * n, 0:n])
        square = big[0:n] + (big[2 * n : 3 * n] + small[0:n])
        mixed = big[n : 2 * n] + (big[3 * n : 4 * n] + small[n : 2 * n])
        eye = ones(iota((n, n), 0) == iota((n, n), 1))
        t_ref[...] = 2.0 * square - eye
        y_ref[...] = 2.0 * (t * y_ref[...] + mixed)
        return 2.0 * t * t - 1.0

    lax.fori_loop(0, steps, step, first)


def kernel(
    pitches,
    field_ref, source_ref, couple_ref, shift_ref, gain_ref, map_ref, slide_ref,
    out_ref,
    f_ref, s_ref, r_ref, cl_ref, cr_ref, smat, ymat, tmat, lhs, rhs, xw_h, xw_l, w_h, w_l, u_ref,
    rmat, yred, tred, yt_h, yt_l, qq, pa, pb, hot, xin,
    edge_send, edge_recv, kq, ab, f63, f63_out, f64, f64_out, c63,
    kq_s, kq_r, ab_s, ab_r, ed_s, ed_r, f63_s, f63_r, fw_s, fw_r, f64_s, f64_r, c63_s, c63_r,
):
    p, q = lax.axis_index("axial"), lax.axis_index("pitch")
    l = lax.rem(p, CHAIN)
    base = p - l
    stator = base > 0
    outlet, inlet = p == CHAIN - 1, p == CHAIN
    zs = pitches // 2
    core = lax.rem(q, 2)
    z = q // 2
    left, right = lax.rem(q + pitches - 1, pitches), lax.rem(q + 1, pitches)

    def at(axial, pitch):
        return {"axial": axial, "pitch": pitch}

    def remote(src, dst, send, recv, axial, pitch):
        return pltpu.make_async_remote_copy(
            src_ref=src, dst_ref=dst, send_sem=send, recv_sem=recv,
            device_id=at(axial, pitch), device_id_type=MESH,
        )

    barrier = pltpu.get_barrier_semaphore()

    def greet(axial, pitch):
        pl.semaphore_signal(barrier, inc=1, device_id=at(axial, pitch), device_id_type=MESH)

    for d in range(1, CHAIN):
        greet(base + lax.rem(l + d, CHAIN), q)
    greet(p, left)
    greet(p, right)

    @pl.when(outlet)
    def _():
        greet(p + 1, q)

    @pl.when(inlet)
    def _():
        for d in range(zs):
            greet(p - 1, 2 * lax.rem(z + d, zs) + core)

    row = iota((NF, 1), 0)
    row_block = jnp.where(row < 245, block_of(row, 7), 0)
    in_sep = jnp.logical_and(row >= NI, row < NI + B)
    row_off = jnp.where(in_sep, row - NI, row - B * row_block)
    row_cell = jnp.where(row < 245, row_block + 1, jnp.where(in_sep, 0, -1))
    lane = iota((1, LINES), 1)

    def stack(dst, src):
        dst[240:NF, :] = jnp.zeros((NF - 240, LINES), F32)
        for m in range(7):
            dst[B * m : B * m + B, :] = src[m + 1]
        dst[NI : NI + B, :] = src[0]

    stack(f_ref, field_ref)

    def place_edges(t):
        pick = jnp.logical_or(
            jnp.logical_and(iota((8, LINES), 0) == 0, iota((8, LINES), 1) == 0),
            jnp.logical_and(iota((8, LINES), 0) == 1, iota((8, LINES), 1) == LINES - 1),
        )
        edge_send[t] = dot(ones(pick), f_ref[...], HIGHEST, ((1,), (1,)))

    place_edges(0)

    pl.semaphore_wait(barrier, CHAIN + 1 + jnp.where(outlet, zs, 0) + jnp.where(inlet, 1, 0))

    def edge_copies(t):
        return (
            remote(edge_send.at[t], edge_recv.at[t, 1], ed_s.at[t, 0], ed_r.at[t, 1], p, left),
            remote(edge_send.at[t], edge_recv.at[t, 0], ed_s.at[t, 1], ed_r.at[t, 0], p, right),
        )

    def f63_copies(t):
        src = field_ref.at[CELLS - 1] if t == 0 else f63_out
        return [
            remote(src, f63.at[t, core, z], f63_s.at[t, d], f63_r.at[t, d], p + 1, 2 * lax.rem(z + d, zs) + core)
            for d in range(zs)
        ]

    def f63_arrivals(t):
        src = field_ref.at[CELLS - 1] if t == 0 else f63_out
        return [
            remote(src, f63.at[t, core, lax.rem(z + zs - d, zs)], f63_s.at[t, d], f63_r.at[t, d], p - 1, q)
            for d in range(zs)
        ]

    def forward_copy(t):
        return remote(f63.at[t, core], f63.at[t, core], fw_s.at[t], fw_r.at[t], p, q + 1 - 2 * core)

    def forward_arrival(t):
        return remote(f63.at[t, 1 - core], f63.at[t, 1 - core], fw_s.at[t], fw_r.at[t], p, q + 1 - 2 * core)

    def f64_copy(t):
        src = field_ref.at[0] if t == 0 else f64_out
        return remote(src, f64.at[t], f64_s.at[t], f64_r.at[t], p - 1, q)

    def f64_arrival(t):
        src = field_ref.at[0] if t == 0 else f64_out
        return remote(src, f64.at[t], f64_s.at[t], f64_r.at[t], p + 1, q)

    def c63_copy(to):
        return remote(couple_ref.at[CELLS - 1], c63, c63_s, c63_r, to, q)

    def kq_copies():
        return [
            remote(kq.at[l], kq.at[l], kq_s.at[d], kq_r.at[d], base + lax.rem(l + d, CHAIN), q)
            for d in range(1, CHAIN)
        ]

    def kq_arrivals():
        peers = [lax.rem(l + CHAIN - d, CHAIN) for d in range(1, CHAIN)]
        return [remote(kq.at[s], kq.at[s], kq_s.at[d + 1], kq_r.at[d + 1], base + s, q) for d, s in enumerate(peers)]

    def ab_copies(t):
        return [
            remote(ab.at[t, l], ab.at[t, l], ab_s.at[t, d], ab_r.at[t, d], base + lax.rem(l + d, CHAIN), q)
            for d in range(1, CHAIN)
        ]

    def ab_arrivals(t):
        peers = [lax.rem(l + CHAIN - d, CHAIN) for d in range(1, CHAIN)]
        return [
            remote(ab.at[t, s], ab.at[t, s], ab_s.at[t, d + 1], ab_r.at[t, d + 1], base + s, q)
            for d, s in enumerate(peers)
        ]

    def send_fields(t):
        @pl.when(outlet)
        def _():
            for copy in f63_copies(t):
                copy.start()

        @pl.when(inlet)
        def _():
            f64_copy(t).start()

        for copy in edge_copies(t):
            copy.start()

    def forward(t):
        @pl.when(inlet)
        def _():
            for copy in f63_arrivals(t):
                copy.wait_recv()
            forward_copy(t).start()

    send_fields(0)

    @pl.when(outlet)
    def _():
        c63_copy(p + 1).start()

    stack(s_ref, source_ref)
    pick_cell = ones(row_cell == iota((NF, CELLS), 1))
    own = row_off == iota((NF, B), 1)
    gain_col = jnp.sum(jnp.where(own, dot(pick_cell, gain_ref[...], HIGHEST), 0.0), 1, keepdims=True)
    shift_col = jnp.sum(jnp.where(own, dot(pick_cell, shift_ref[...], HIGHEST), 0.0), 1, keepdims=True)
    g_col = shift_col + 2.0 * gain_col

    @pl.when(inlet)
    def _():
        lines = map_ref[pl.ds(q, 1), :]
        xin[...] = jnp.zeros_like(xin)
        for a in range(INST):
            found = lax.rem(lines + slide_ref[a], pitches * LINES)
            hot[a] = ones(iota((LINES, LINES), 0) == lax.rem(found, LINES)).astype(BF16)

    cl_ref[240:NI, :] = jnp.zeros((NI - 240, B), F32)
    cr_ref[240:NI, :] = jnp.zeros((NI - 240, B), F32)
    for m in range(7):
        cl_ref[B * m : B * m + B, :] = couple_ref[m]
        cr_ref[B * m : B * m + B, :] = couple_ref[m + 1]
    col = iota((1, NI), 1)
    col_block = block_of(col, 8)
    tile = ones(iota((B, NI), 0) == col - B * col_block)
    rep_l = dot(cl_ref[...], tile, HIGHEST)
    rep_r = dot(cr_ref[...], tile, HIGHEST)
    in_block = block_of(iota((NI, 1), 0), 8)
    mid, half, first, scale = plan(local_bounds(), LOCAL_STEPS)
    g_in = g_col[0:NI]
    same = iota((NI, NI), 0) == iota((NI, NI), 1)
    s_full = jnp.where(in_block == col_block, rep_l + rep_r, 0.0)
    s_full -= jnp.where(col_block == in_block + 1, rep_r, 0.0)
    s_full -= jnp.where(col_block + 1 == in_block, rep_l, 0.0)
    s_full += jnp.where(same, jnp.where(iota((NI, 1), 0) < 245, g_in, mid), 0.0)
    s_full = jnp.where(jnp.logical_and(in_block == 7, jnp.logical_not(same)), 0.0, s_full)
    s_full = jnp.where(jnp.logical_and(col_block == 7, jnp.logical_not(same)), 0.0, s_full)
    smat[...] = s_full
    tmat[...] = jnp.where(same, mid - s_full, -s_full) * (1.0 / half)
    ymat[...] = jnp.where(same, 1.0 / half, 0.0)
    links = jnp.where(jnp.logical_and(in_block == 0, col_block == 0), rep_l, 0.0)
    links += jnp.where(jnp.logical_and(in_block == 6, col_block == 1), rep_r, 0.0)
    links = links[:, 0:128]
    links += jnp.where(iota((NI, 128), 1) == row_off[0:NI] + 2 * B, g_in, 0.0)
    chebyshev(NI, 0, jnp.asarray(first, F32), lhs, rhs, ymat, tmat, LOCAL_STEPS)
    x0 = ymat[...] * scale
    ymat[...] = x0
    rest = jnp.where(same, 1.0, 0.0) - dot(smat[...], ymat[...], HIGHEST)
    inv = x0 + dot(x0.astype(BF16), rest.astype(BF16))
    ymat[...] = inv
    forward(0)
    w = dot(ymat[...], links, HIGHEST)
    xw_h[0:NI], xw_l[0:NI] = split(inv)
    xw_h[NI:NF], xw_l[NI:NF] = split(w.T)
    w_h[...], w_l[...] = split(w)
    u_ref[...] = dot(links.T, w, HIGHEST)

    fr, to = iota((128, 128), 0), iota((128, 128), 1)
    top = ones(jnp.logical_or(
        jnp.logical_and(to < B, jnp.logical_or(fr == to + B, fr == to + 2 * B)),
        jnp.logical_and(jnp.logical_and(to >= B, to < 2 * B), fr == to),
    ))
    low = ones(jnp.logical_and(
        jnp.logical_and(to >= 2 * B, to < 3 * B), jnp.logical_or(fr == to - 2 * B, fr == to)
    ))
    sep_g = g_col[NI : NI + 40]
    part = dot(u_ref[0:40, :], top, HIGHEST) + dot(u_ref[B : B + 40, :], low, HIGHEST)
    part += jnp.where(iota((40, 128), 0) == iota((40, 128), 1), sep_g, 0.0)
    kq[l] = part

    @pl.when(inlet)
    def _():
        c63_copy(p - 1).wait_recv()
        kq[l, 0:B, 0:B] = kq[l, 0:B, 0:B] + c63[...]

    for copy in kq_copies():
        copy.start()

    def right_side(t):
        for copy in reversed(edge_copies(t)):
            copy.wait_recv()
        spot = jnp.logical_or(
            jnp.logical_and(iota((16, LINES), 0) == 1, iota((16, LINES), 1) == 0),
            jnp.logical_and(iota((16, LINES), 0) == 8, iota((16, LINES), 1) == LINES - 1),
        )
        sides = dot(edge_recv[t].reshape(16, NF), ones(spot), HIGHEST, ((0,), (0,)))
        f = f_ref[...]
        near = jnp.where(lane == 0, 0.0, pltpu.roll(f, 1, 1)) + jnp.where(
            lane == LINES - 1, 0.0, pltpu.roll(f, LINES - 1, 1)
        )
        r_ref[...] = s_ref[...] + gain_col * (near + sides)

        @pl.when(outlet)
        def _():
            f64_arrival(t).wait_recv()
            r_ref[210:245, :] = r_ref[210:245, :] + dot(couple_ref[CELLS - 1], f64[t], HIGHEST)

    def reach(t):
        forward_arrival(t).wait_recv()
        lines = map_ref[pl.ds(q, 1), :]
        pieces = []
        for a in range(INST):
            for c in range(2):
                xin[a, :, c, 0:VARS, :] = f63[t, c, :, VARS * a : VARS * a + VARS, :]
            high, low_part = split(xin[a].reshape(pitches * 8, LINES))
            found = lax.rem(lines + slide_ref[a], pitches * LINES) // LINES
            got = (dot(high, hot[a]) + dot(low_part, hot[a])).reshape(pitches, 8, LINES)
            which = iota((pitches, 1, LINES), 0) == found.reshape(1, 1, LINES)
            pieces.append(jnp.sum(jnp.where(which, got, 0.0), 0)[0:VARS])
        for a in range(INST):
            u_ref[VARS * a : VARS * a + VARS, :] = pieces[a]
        return dot(c63[...], u_ref[0:B, :], HIGHEST)

    def send_sides(t):
        rh, rl = split(r_ref[0:NI, :])
        both = dot3((xw_h[...], xw_l[...]), (rh, rl))
        r_ref[0:NI, :] = both[0:NI]
        ends = both[NI:NF] + r_ref[NI:NF, :]
        ab[t, l] = ends[0:72]

        @pl.when(inlet)
        def _():
            ab[t, l, 0:B, :] = ab[t, l, 0:B, :] + reach(t)

        for copy in ab_copies(t):
            copy.start()

    def finish(t):
        for copy in ab_arrivals(t):
            copy.wait_recv()
        pb[0:B, :] = jnp.zeros((B, LINES), F32)
        pa[B * CHAIN : NR, :] = jnp.zeros((NR - B * CHAIN, LINES), F32)
        for s in range(CHAIN):
            pa[B * s : B * s + B, :] = ab[t, s, 0:B, :]
            pb[B * s + B : B * s + 2 * B, :] = ab[t, s, B : 2 * B, :]
        ends = dot3((yt_h[...], yt_l[...]), split(pa[...] + pb[0:NR, :]))
        f_ref[0:NI, :] = r_ref[0:NI, :] + dot3((w_h[...], w_l[...]), split(ends))
        f_ref[NI:NF, :] = ends

    right_side(0)
    send_sides(0)

    for copy in kq_arrivals():
        copy.wait_recv()
    qq[0:B, 128:256] = jnp.zeros((B, 128), F32)
    qq[B * CHAIN : NR, :] = jnp.zeros((NR - B * CHAIN, 256), F32)
    for s in range(CHAIN):
        qq[B * s : B * s + B, 0:128] = kq[s, 0:B, :]
        if s + 1 < CHAIN:
            qq[B * s + B : B * s + 2 * B, 128:256] = kq[s, 0:B, :]
    rcol, rrow = iota((1, NR), 1), iota((NR, 1), 0)
    rcol_block, rrow_block = block_of(rcol, 9), block_of(rrow, 9)
    rcol_off, rrow_off = rcol - B * rcol_block, rrow - B * rrow_block
    source_row = iota((256, NR), 0)
    diag_tile = ones(jnp.logical_or(source_row == rcol_off, source_row == rcol_off + 128 + 2 * B))
    link_tile = ones(iota((128, NR), 0) == rcol_off + B)
    link_turn = ones(iota((NR, 128), 1) == rrow_off + B)
    diag = dot(qq[...], diag_tile, HIGHEST)
    above = dot(qq[:, 0:128], link_tile, HIGHEST)
    below = dot(link_turn, qq[:, 0:128], HIGHEST, ((1,), (1,)))
    rotor_plan, stator_plan = plan(scalar_bounds(False), REDUCED_STEPS), plan(scalar_bounds(True), REDUCED_STEPS)
    mid, half_inv, first, scale = (
        jnp.where(stator, jnp.asarray(b, F32), jnp.asarray(a, F32))
        for a, b in zip(
            (rotor_plan[0], 1.0 / rotor_plan[1], rotor_plan[2], rotor_plan[3]),
            (stator_plan[0], 1.0 / stator_plan[1], stator_plan[2], stator_plan[3]),
        )
    )
    same = iota((NR, NR), 0) == iota((NR, NR), 1)
    live = jnp.logical_and(rrow_block < CHAIN, rcol_block < CHAIN)
    red = jnp.where(rcol_block == rrow_block, diag, 0.0)
    red -= jnp.where(rcol_block == rrow_block + 1, above, 0.0)
    red -= jnp.where(rcol_block + 1 == rrow_block, below, 0.0)
    red = jnp.where(live, red, jnp.where(same, mid, 0.0))
    rmat[...] = red
    tred[...] = jnp.where(same, mid - red, -red) * half_inv
    yred[...] = jnp.where(same, half_inv, 0.0)
    chebyshev(NR, 0, first, lhs, rhs, yred, tred, REDUCED_STEPS)
    xr = yred[...] * scale
    want = jnp.logical_and(
        jnp.logical_and(iota((128, NR), 1) == iota((128, NR), 0) + B * l, iota((128, NR), 0) < 2 * B),
        iota((128, NR), 1) < B * CHAIN,
    )
    wanted = ones(want)
    xh, xl = split(xr)
    wanted_b = wanted.astype(BF16)
    y0 = dot(wanted_b, xh) + dot(wanted_b, xl)
    rest = wanted - dot(y0, rmat[...], HIGHEST)
    yt_h[...], yt_l[...] = split(y0 + dot(rest.astype(BF16), xh))

    finish(0)

    f63_out[...] = f_ref[210:245, :]
    f64_out[...] = f_ref[NI : NI + B, :]
    place_edges(1)
    send_fields(1)
    right_side(1)
    forward(1)
    send_sides(1)
    finish(1)
    out_ref[0] = f_ref[NI : NI + B, :]
    for m in range(7):
        out_ref[m + 1] = f_ref[B * m : B * m + B, :]

    for t in range(2):
        for copy in edge_copies(t) + tuple(ab_copies(t)):
            copy.wait_send()
    for copy in kq_copies():
        copy.wait_send()

    @pl.when(outlet)
    def _():
        for t in range(2):
            for copy in f63_copies(t):
                copy.wait_send()
        c63_copy(p + 1).wait_send()

    @pl.when(inlet)
    def _():
        for t in range(2):
            forward_copy(t).wait_send()
            f64_copy(t).wait_send()


def body(pitches, field, source, couple, shift, gain, row_map, slide):
    zs = pitches // 2
    vmem = pl.BlockSpec(memory_space=pltpu.VMEM)
    dma = pltpu.SemaphoreType.DMA
    V = pltpu.VMEM
    return pl.pallas_call(
        functools.partial(kernel, pitches),
        out_shape=jax.ShapeDtypeStruct(field.shape, F32),
        in_specs=[vmem] * 6 + [pl.BlockSpec(memory_space=pltpu.SMEM)],
        out_specs=vmem,
        scratch_shapes=[
            V((NF, LINES), F32), V((NF, LINES), F32), V((NF, LINES), F32),
            V((NI, B), F32), V((NI, B), F32),
            V((NI, NI), F32), V((NI, NI), F32), V((NI, NI), F32),
            V((4 * NR, NR), BF16), V((2 * NR, NR), BF16),
            V((NF, NI), BF16), V((NF, NI), BF16),
            V((NI, 128), BF16), V((NI, 128), BF16),
            V((128, 128), F32),
            V((NR, NR), F32), V((NR, NR), F32), V((NR, NR), F32),
            V((128, NR), BF16), V((128, NR), BF16),
            V((NR, 256), F32),
            V((NR, LINES), F32), V((B * (CHAIN + 1) + 5, LINES), F32),
            V((INST, LINES, LINES), BF16),
            V((INST, zs, 2, 8, LINES), F32),
            V((2, 8, NF), F32), V((2, 2, 8, NF), F32),
            V((CHAIN, 40, 128), F32),
            V((2, CHAIN, 72, LINES), F32),
            V((2, 2, zs, B, LINES), F32), V((B, LINES), F32),
            V((2, B, LINES), F32), V((B, LINES), F32),
            V((B, B), F32),
            dma((CHAIN,)), dma((CHAIN,)), dma((2, CHAIN)), dma((2, CHAIN)),
            dma((2, 2)), dma((2, 2)), dma((2, zs)), dma((2, zs)),
            dma((2,)), dma((2,)), dma((2,)), dma((2,)), dma, dma,
        ],
        compiler_params=pltpu.CompilerParams(
            collective_id=0, has_side_effects=True, vmem_limit_bytes=48 * 2**20
        ),
        name="sweeps",
    )(field, source, couple, shift, gain, row_map.reshape(pitches, LINES), slide)


def solution(mesh):
    return jax.shard_map(
        functools.partial(body, mesh.shape["pitch"]),
        mesh=mesh,
        in_specs=(
            P("axial", None, "pitch"),
            P("axial", None, "pitch"),
            P("axial", None, None),
            P("axial", None),
            P("axial", None),
            P(),
            P(),
        ),
        out_specs=P("axial", None, "pitch"),
        check_vma=False,
    )
```

```python
import functools
import math

import jax
import jax.numpy as jnp
import numpy as np
from jax import lax
from jax.experimental import pallas as pl
from jax.experimental.pallas import tpu as pltpu
from jax.sharding import PartitionSpec as P

INST, VARS, B = 7, 5, 35
CELLS, LINES, CHAIN = 8, 128, 8
NI = 256
NR = 288
NF = 384
F32, BF16, I32 = jnp.float32, jnp.bfloat16, jnp.int32
HIGHEST = lax.Precision.HIGHEST
MESH = pl.DeviceIdType.MESH

C_LOW, C_HIGH, G_LOW, G_HIGH = 0.299, 5.51, 0.00109, 0.00352
LOCAL_STEPS, REDUCED_STEPS = 7, 6
FIRST_SCALE = 0.5


def scalar_bounds(stator):
    ends = []
    for c, g in ((C_LOW, G_LOW), (C_HIGH, G_HIGH)):
        n = CELLS * CHAIN
        t = np.diag(np.full(n, 2 * c + g)) - c * np.eye(n, k=1) - c * np.eye(n, k=-1)
        if not stator:
            t[0, 0] -= c
        keep = np.arange(0, n, CELLS)
        scale = np.where(np.arange(CHAIN) == 0, FIRST_SCALE if stator else 1.0, 1.0)
        rest = np.setdiff1d(np.arange(n), keep)
        s = t[np.ix_(keep, keep)] - t[np.ix_(keep, rest)] @ np.linalg.solve(
            t[np.ix_(rest, rest)], t[np.ix_(rest, keep)]
        )
        ends.append(np.linalg.eigvalsh(scale[:, None] * s * scale[None, :]))
    return float(ends[0][0]), float(ends[1][-1])


def local_bounds():
    bend = 2 * math.cos(math.pi / CELLS)
    return C_LOW * (2 - bend) + G_LOW, C_HIGH * (2 + bend) + G_HIGH


def plan(bounds, steps):
    low, high = bounds
    mid, half = 0.5 * (high + low), 0.5 * (high - low)
    t = first = mid / half
    for _ in range(steps):
        t = 2 * t * t - 1
    return mid, half, first, 1.0 / t


def dot(a, b, precision=None, dims=((1,), (0,))):
    return lax.dot_general(a, b, (dims, ((), ())), precision=precision, preferred_element_type=F32)


def split(x):
    high = x.astype(BF16)
    return high, (x - high.astype(F32)).astype(BF16)


def dot3(a, b):
    (ah, al), (bh, bl) = a, b
    return dot(ah, bh) + (dot(ah, bl) + dot(al, bh))


def iota(shape, axis):
    return lax.broadcasted_iota(I32, shape, axis)


def block_of(index, count):
    return sum(((index >= B * k).astype(I32) for k in range(1, count)), jnp.zeros_like(index))


def ones(mask):
    return jnp.where(mask, 1.0, 0.0).astype(F32)


def chebyshev(n, t, half_inv, lhs, rhs, y_ref, t_ref, steps, exact):
    eye = ones(iota((n, n), 0) == iota((n, n), 1))
    rows = 4 if exact else 3

    def load(with_y):
        th, tl = split(t_ref[...])
        lhs[0:n, 0:n] = th
        lhs[n : 2 * n, 0:n] = tl
        rhs[0:n, 0:n] = th
        rhs[n : 2 * n, 0:n] = tl
        if with_y and exact:
            lhs[2 * n : 3 * n, 0:n], lhs[3 * n : 4 * n, 0:n] = split(y_ref[...])
        elif with_y:
            lhs[2 * n : 3 * n, 0:n] = y_ref[...].astype(BF16)

    load(False)
    big = dot(lhs[0 : 2 * n, 0:n], rhs[0:n, 0:n])
    square = big[0:n] + (big[n : 2 * n] + dot(lhs[0:n, 0:n], rhs[n : 2 * n, 0:n]))
    y_ref[...] = (2.0 * half_inv) * (t * eye + t_ref[...])
    t_ref[...] = 2.0 * square - eye
    t = 2.0 * t * t - 1.0

    def step(_, t):
        load(True)
        big = dot(lhs[0 : rows * n, 0:n], rhs[0:n, 0:n])
        square = big[0:n] + (big[n : 2 * n] + dot(lhs[0:n, 0:n], rhs[n : 2 * n, 0:n]))
        mixed = big[2 * n : 3 * n]
        if exact:
            mixed += big[3 * n : 4 * n] + dot(lhs[2 * n : 3 * n, 0:n], rhs[n : 2 * n, 0:n])
        t_ref[...] = 2.0 * square - eye
        y_ref[...] = 2.0 * (t * y_ref[...] + mixed)
        return 2.0 * t * t - 1.0

    t = lax.fori_loop(0, steps - 2, step, t)
    load(True)
    big = dot(lhs[2 * n : rows * n, 0:n], rhs[0:n, 0:n])
    mixed = big[0:n]
    if exact:
        mixed += big[n : 2 * n] + dot(lhs[2 * n : 3 * n, 0:n], rhs[n : 2 * n, 0:n])
    y_ref[...] = 2.0 * (t * y_ref[...] + mixed)


def kernel(
    pitches,
    *refs,
):
    args, (out_ref, *args_v) = refs[:7], refs[7:15]
    (
        f_ref, s_ref, r_ref, cl_ref, cr_ref, smat, ymat, tmat, lhs, rhs, xw_h, xw_l, w_h, w_l, u_ref,
        rmat, yred, tred, yt_h, yt_l, qq, pa, pb, hot, xin,
        edge_send, edge_recv, kq, ab, f63, f63_out, f64, f64_out, c63, c63_out, late,
        kq_s, kq_r, ab_s, ab_r, ed_s, ed_r, f63_s, f63_r, fw_s, fw_r, f64_s, f64_r, c63_s, c63_r, late_s, late_r, in_s,
    ) = refs[15:]
    field_v, source_v, couple_v, shift_v, gain_v, map_v, slide_v = args_v
    p, q = lax.axis_index("axial"), lax.axis_index("pitch")
    l = lax.rem(p, CHAIN)
    base = p - l
    stator = base > 0
    outlet, inlet = p == CHAIN - 1, p == CHAIN
    zs = pitches // 2
    core = lax.rem(q, 2)
    z = q // 2
    left, right = lax.rem(q + pitches - 1, pitches), lax.rem(q + 1, pitches)

    def at(axial, pitch):
        return {"axial": axial, "pitch": pitch}

    def remote(src, dst, send, recv, axial, pitch):
        return pltpu.make_async_remote_copy(
            src_ref=src, dst_ref=dst, send_sem=send, recv_sem=recv,
            device_id=at(axial, pitch), device_id_type=MESH,
        )

    loads = [pltpu.make_async_copy(args[i], args_v[i], in_s.at[i]) for i in range(7)]
    for load in loads:
        load.start()

    barrier = pltpu.get_barrier_semaphore()

    def greet(axial, pitch):
        pl.semaphore_signal(barrier, inc=1, device_id=at(axial, pitch), device_id_type=MESH)

    for d in range(1, CHAIN):
        greet(base + lax.rem(l + d, CHAIN), q)
    greet(p, left)
    greet(p, right)

    @pl.when(outlet)
    def _():
        greet(p + 1, q)

    @pl.when(inlet)
    def _():
        for d in range(zs):
            greet(p - 1, 2 * lax.rem(z + d, zs) + core)

    row = iota((NF, 1), 0)
    row_block = jnp.where(row < 245, block_of(row, 7), 0)
    in_sep = jnp.logical_and(row >= NI, row < NI + B)
    row_off = jnp.where(in_sep, row - NI, row - B * row_block)
    row_cell = jnp.where(row < 245, row_block + 1, jnp.where(in_sep, 0, -1))
    lane = iota((1, LINES), 1)

    def cell_of(src, i):
        return src[pl.ds(i, B, stride=CELLS), :]

    def stack(dst, src):
        dst[240:NF, :] = jnp.zeros((NF - 240, LINES), F32)
        for m in range(7):
            dst[B * m : B * m + B, :] = cell_of(src, m + 1)
        dst[NI : NI + B, :] = cell_of(src, 0)

    loads[0].wait()
    stack(f_ref, field_v)
    f63_out[0] = cell_of(field_v, CELLS - 1)
    f64_out[0] = cell_of(field_v, 0)
    loads[2].wait()
    c63_out[...] = cell_of(couple_v, CELLS - 1)

    def place_edges(t):
        pick = jnp.logical_or(
            jnp.logical_and(iota((8, LINES), 0) == 0, iota((8, LINES), 1) == 0),
            jnp.logical_and(iota((8, LINES), 0) == 1, iota((8, LINES), 1) == LINES - 1),
        )
        edge_send[t] = dot(ones(pick), f_ref[...], HIGHEST, ((1,), (1,)))

    place_edges(0)
    for i in (1, 3, 4, 5, 6):
        loads[i].wait()
    pl.semaphore_wait(barrier, CHAIN + 1 + jnp.where(outlet, zs, 0) + jnp.where(inlet, 1, 0))

    def edge_copies(t):
        return (
            remote(edge_send.at[t], edge_recv.at[t, 1], ed_s.at[t, 0], ed_r.at[t, 1], p, left),
            remote(edge_send.at[t], edge_recv.at[t, 0], ed_s.at[t, 1], ed_r.at[t, 0], p, right),
        )

    def f63_copies(t):
        src = f63_out.at[t]
        return [
            remote(src, f63.at[t, core, z], f63_s.at[t, d], f63_r.at[t, d], p + 1, 2 * lax.rem(z + d, zs) + core)
            for d in range(zs)
        ]

    def f63_arrivals(t):
        src = f63_out.at[t]
        return [
            remote(src, f63.at[t, core, lax.rem(z + zs - d, zs)], f63_s.at[t, d], f63_r.at[t, d], p - 1, q)
            for d in range(zs)
        ]

    def forward_copy(t):
        return remote(f63.at[t, core], f63.at[t, core], fw_s.at[t], fw_r.at[t], p, q + 1 - 2 * core)

    def forward_arrival(t):
        return remote(f63.at[t, 1 - core], f63.at[t, 1 - core], fw_s.at[t], fw_r.at[t], p, q + 1 - 2 * core)

    def f64_copy(t):
        src = f64_out.at[t]
        return remote(src, f64.at[t], f64_s.at[t], f64_r.at[t], p - 1, q)

    def f64_arrival(t):
        src = f64_out.at[t]
        return remote(src, f64.at[t], f64_s.at[t], f64_r.at[t], p + 1, q)

    def c63_copy(to):
        return remote(c63_out, c63, c63_s, c63_r, to, q)

    def kq_copies():
        return [
            remote(kq.at[l], kq.at[l], kq_s.at[d], kq_r.at[d], base + lax.rem(l + d, CHAIN), q)
            for d in range(1, CHAIN)
        ]

    def kq_arrivals():
        peers = [lax.rem(l + CHAIN - d, CHAIN) for d in range(1, CHAIN)]
        return [remote(kq.at[s], kq.at[s], kq_s.at[d + 1], kq_r.at[d + 1], base + s, q) for d, s in enumerate(peers)]

    def ab_copies(t):
        return [
            remote(ab.at[t, l], ab.at[t, l], ab_s.at[t, d], ab_r.at[t, d], base + lax.rem(l + d, CHAIN), q)
            for d in range(1, CHAIN)
        ]

    def ab_arrivals(t):
        peers = [lax.rem(l + CHAIN - d, CHAIN) for d in range(1, CHAIN)]
        return [
            remote(ab.at[t, s], ab.at[t, s], ab_s.at[t, d + 1], ab_r.at[t, d + 1], base + s, q)
            for d, s in enumerate(peers)
        ]

    def send_inlet(t):
        @pl.when(inlet)
        def _():
            f64_copy(t).start()

    def send_outlet(t):
        @pl.when(outlet)
        def _():
            for copy in f63_copies(t):
                copy.start()

    def send_edges(t):
        for copy in edge_copies(t):
            copy.start()

    def late_copies(t):
        return [
            remote(late.at[t], late.at[t], late_s.at[t, d], late_r.at[t], base + lax.rem(l + d, CHAIN), q)
            for d in range(1, CHAIN)
        ]

    def late_arrival(t):
        return remote(late.at[t], late.at[t], late_s.at[t, 0], late_r.at[t], base, q)

    def forward(t):
        @pl.when(inlet)
        def _():
            for copy in f63_arrivals(t):
                copy.wait_recv()
            forward_copy(t).start()

    send_outlet(0)
    send_inlet(0)
    send_edges(0)

    @pl.when(outlet)
    def _():
        c63_copy(p + 1).start()

    stack(s_ref, source_v)
    pick_cell = ones(row_cell == iota((NF, CELLS), 1))
    own = row_off == iota((NF, B), 1)
    gain_col = jnp.sum(jnp.where(own, dot(pick_cell, gain_v[...], HIGHEST), 0.0), 1, keepdims=True)
    shift_col = jnp.sum(jnp.where(own, dot(pick_cell, shift_v[...], HIGHEST), 0.0), 1, keepdims=True)
    g_col = shift_col + 2.0 * gain_col

    @pl.when(inlet)
    def _():
        lines = map_v[pl.ds(q, 1), :]
        xin[...] = jnp.zeros_like(xin)
        for a in range(INST):
            found = lax.rem(lines + slide_v[:, a : a + 1], pitches * LINES)
            hot[a] = ones(iota((LINES, LINES), 0) == lax.rem(found, LINES)).astype(BF16)

    cl_ref[240:NI, :] = jnp.zeros((NI - 240, B), F32)
    cr_ref[240:NI, :] = jnp.zeros((NI - 240, B), F32)
    for m in range(7):
        cl_ref[B * m : B * m + B, :] = cell_of(couple_v, m)
        cr_ref[B * m : B * m + B, :] = cell_of(couple_v, m + 1)
    col = iota((1, NI), 1)
    col_block = block_of(col, 8)
    tile = ones(iota((B, NI), 0) == col - B * col_block)
    rep_l = dot(cl_ref[...], tile, HIGHEST)
    rep_r = dot(cr_ref[...], tile, HIGHEST)
    in_block = block_of(iota((NI, 1), 0), 8)
    mid, half, first, scale = plan(local_bounds(), LOCAL_STEPS)
    g_in = g_col[0:NI]
    same = iota((NI, NI), 0) == iota((NI, NI), 1)
    s_full = jnp.where(in_block == col_block, rep_l + rep_r, 0.0)
    s_full -= jnp.where(col_block == in_block + 1, rep_r, 0.0)
    s_full -= jnp.where(col_block + 1 == in_block, rep_l, 0.0)
    s_full += jnp.where(same, jnp.where(iota((NI, 1), 0) < 245, g_in, mid), 0.0)
    s_full = jnp.where(jnp.logical_and(in_block == 7, jnp.logical_not(same)), 0.0, s_full)
    s_full = jnp.where(jnp.logical_and(col_block == 7, jnp.logical_not(same)), 0.0, s_full)
    smat[...] = s_full
    tmat[...] = jnp.where(same, mid - s_full, -s_full) * (1.0 / half)
    links = jnp.where(jnp.logical_and(in_block == 0, col_block == 0), rep_l, 0.0)
    links += jnp.where(jnp.logical_and(in_block == 6, col_block == 1), rep_r, 0.0)
    links = links[:, 0:128]
    links += jnp.where(iota((NI, 128), 1) == row_off[0:NI] + 2 * B, g_in, 0.0)
    chebyshev(NI, jnp.asarray(first, F32), 1.0 / half, lhs, rhs, ymat, tmat, LOCAL_STEPS, True)
    x0 = ymat[...] * scale
    ymat[...] = x0
    rest = jnp.where(same, 1.0, 0.0) - dot(smat[...], ymat[...], HIGHEST)
    inv = x0 + dot(x0.astype(BF16), rest.astype(BF16))
    ymat[...] = inv
    forward(0)
    w = dot(ymat[...], links, HIGHEST)
    xw_h[0:NI], xw_l[0:NI] = split(inv)
    xw_h[NI:NF], xw_l[NI:NF] = split(w.T)
    w_h[...], w_l[...] = split(w)
    u_ref[...] = dot(links.T, w, HIGHEST)

    fr, to = iota((128, 128), 0), iota((128, 128), 1)
    top = ones(jnp.logical_or(
        jnp.logical_and(to < B, jnp.logical_or(fr == to + B, fr == to + 2 * B)),
        jnp.logical_and(jnp.logical_and(to >= B, to < 2 * B), fr == to),
    ))
    low = ones(jnp.logical_and(
        jnp.logical_and(to >= 2 * B, to < 3 * B), jnp.logical_or(fr == to - 2 * B, fr == to)
    ))
    sep_g = g_col[NI : NI + 40]
    part = dot(u_ref[0:40, :], top, HIGHEST) + dot(u_ref[B : B + 40, :], low, HIGHEST)
    part += jnp.where(iota((40, 128), 0) == iota((40, 128), 1), sep_g, 0.0)
    kq[l] = part

    @pl.when(inlet)
    def _():
        c63_copy(p - 1).wait_recv()
        kq[l, 0:B, 0:B] = kq[l, 0:B, 0:B] + c63[...]

    for copy in kq_copies():
        copy.start()

    def right_side(t):
        for copy in reversed(edge_copies(t)):
            copy.wait_recv()
        spot = jnp.logical_or(
            jnp.logical_and(iota((16, LINES), 0) == 1, iota((16, LINES), 1) == 0),
            jnp.logical_and(iota((16, LINES), 0) == 8, iota((16, LINES), 1) == LINES - 1),
        )
        sides = dot(edge_recv[t].reshape(16, NF), ones(spot), HIGHEST, ((0,), (0,)))
        f = f_ref[...]
        near = jnp.where(lane == 0, 0.0, pltpu.roll(f, 1, 1)) + jnp.where(
            lane == LINES - 1, 0.0, pltpu.roll(f, LINES - 1, 1)
        )
        r_ref[...] = s_ref[...] + gain_col * (near + sides)

        @pl.when(outlet)
        def _():
            f64_arrival(t).wait_recv()
            r_ref[210:245, :] = r_ref[210:245, :] + dot(c63_out[...], f64[t], HIGHEST)

    def reach(t):
        lines = map_v[pl.ds(q, 1), :]
        total = [None] * INST
        for half_at in range(2):
            c = core if half_at == 0 else 1 - core
            if half_at == 1:
                forward_arrival(t).wait_recv()
            for a in range(INST):
                xin[a, :, 0:VARS, :] = f63[t, c, :, VARS * a : VARS * a + VARS, :]
            for a in range(INST):
                high, low_part = split(xin[a].reshape(zs * 8, LINES))
                found = lax.rem(lines + slide_v[:, a : a + 1], pitches * LINES) // LINES
                got = (dot(high, hot[a]) + dot(low_part, hot[a])).reshape(zs, 8, LINES)
                which = 2 * iota((zs, 1, LINES), 0) + c == found.reshape(1, 1, LINES)
                piece = jnp.sum(jnp.where(which, got, 0.0), 0)[0:VARS]
                total[a] = piece if half_at == 0 else total[a] + piece
        for a in range(INST):
            u_ref[VARS * a : VARS * a + VARS, :] = total[a]
        late[t] = dot(c63[...], u_ref[0:B, :], HIGHEST)
        for copy in late_copies(t):
            copy.start()

    def send_sides(t):
        rh, rl = split(r_ref[0:NI, :])
        both = dot3((xw_h[...], xw_l[...]), (rh, rl))
        r_ref[0:NI, :] = both[0:NI]
        ends = both[NI:NF] + r_ref[NI:NF, :]
        ab[t, l] = ends[0:72]
        for copy in ab_copies(t):
            copy.start()

    def finish(t):
        for copy in ab_arrivals(t):
            copy.wait_recv()
        pb[0:B, :] = jnp.zeros((B, LINES), F32)
        pa[B * CHAIN : NR, :] = jnp.zeros((NR - B * CHAIN, LINES), F32)
        for s in range(CHAIN):
            pa[B * s : B * s + B, :] = ab[t, s, 0:B, :]
            pb[B * s + B : B * s + 2 * B, :] = ab[t, s, B : 2 * B, :]

        @pl.when(stator)
        def _():
            @pl.when(jnp.logical_not(inlet))
            def _():
                late_arrival(t).wait_recv()

            pa[0:B, :] = pa[0:B, :] + late[t]

        ends = dot3((yt_h[...], yt_l[...]), split(pa[...] + pb[0:NR, :]))
        if t == 0:
            f64_out[1] = ends[0:B]
            send_inlet(1)
        f_ref[0:NI, :] = r_ref[0:NI, :] + dot3((w_h[...], w_l[...]), split(ends))
        f_ref[NI:NF, :] = ends

    right_side(0)
    send_sides(0)

    @pl.when(inlet)
    def _():
        reach(0)

    for copy in kq_arrivals():
        copy.wait_recv()
    qq[0:B, 128:256] = jnp.zeros((B, 128), F32)
    qq[B * CHAIN : NR, :] = jnp.zeros((NR - B * CHAIN, 256), F32)
    for s in range(CHAIN):
        qq[B * s : B * s + B, 0:128] = kq[s, 0:B, :]
        if s + 1 < CHAIN:
            qq[B * s + B : B * s + 2 * B, 128:256] = kq[s, 0:B, :]
    rcol, rrow = iota((1, NR), 1), iota((NR, 1), 0)
    rcol_block, rrow_block = block_of(rcol, 9), block_of(rrow, 9)
    rcol_off, rrow_off = rcol - B * rcol_block, rrow - B * rrow_block
    source_row = iota((256, NR), 0)
    diag_tile = ones(jnp.logical_or(source_row == rcol_off, source_row == rcol_off + 128 + 2 * B))
    link_tile = ones(iota((128, NR), 0) == rcol_off + B)
    link_turn = ones(iota((NR, 128), 1) == rrow_off + B)
    diag = dot(qq[...], diag_tile, HIGHEST)
    above = dot(qq[:, 0:128], link_tile, HIGHEST)
    below = dot(link_turn, qq[:, 0:128], HIGHEST, ((1,), (1,)))
    rotor_plan, stator_plan = plan(scalar_bounds(False), REDUCED_STEPS), plan(scalar_bounds(True), REDUCED_STEPS)
    mid, half_inv, first, scale = (
        jnp.where(stator, jnp.asarray(b, F32), jnp.asarray(a, F32))
        for a, b in zip(
            (rotor_plan[0], 1.0 / rotor_plan[1], rotor_plan[2], rotor_plan[3]),
            (stator_plan[0], 1.0 / stator_plan[1], stator_plan[2], stator_plan[3]),
        )
    )
    same = iota((NR, NR), 0) == iota((NR, NR), 1)
    live = jnp.logical_and(rrow_block < CHAIN, rcol_block < CHAIN)
    red = jnp.where(rcol_block == rrow_block, diag, 0.0)
    red -= jnp.where(rcol_block == rrow_block + 1, above, 0.0)
    red -= jnp.where(rcol_block + 1 == rrow_block, below, 0.0)
    first_scale = jnp.where(stator, jnp.asarray(FIRST_SCALE, F32), jnp.asarray(1.0, F32))
    row_scale, col_scale = (jnp.where(i < B, first_scale, 1.0) for i in (rrow, rcol))
    red = jnp.where(live, red * (row_scale * col_scale), jnp.where(same, mid, 0.0))
    rmat[...] = red
    tred[...] = jnp.where(same, mid - red, -red) * half_inv
    chebyshev(NR, first, half_inv, lhs, rhs, yred, tred, REDUCED_STEPS, False)
    xr = yred[...] * scale
    want = jnp.logical_and(
        jnp.logical_and(iota((128, NR), 1) == iota((128, NR), 0) + B * l, iota((128, NR), 0) < 2 * B),
        iota((128, NR), 1) < B * CHAIN,
    )
    wanted = jnp.where(want, col_scale, 0.0)
    yred[...] = xr
    y = dot3(split(wanted), split(yred[...]))
    for _ in range(2):
        rest = wanted - dot(y, rmat[...], HIGHEST)
        y += dot(rest.astype(BF16), yred[...].astype(BF16))
    yt_h[...], yt_l[...] = split(y * col_scale)

    finish(0)

    f63_out[1] = f_ref[210:245, :]
    send_outlet(1)
    place_edges(1)
    send_edges(1)
    right_side(1)
    send_sides(1)
    forward(1)

    @pl.when(inlet)
    def _():
        reach(1)

    finish(1)
    out_ref[pl.ds(0, B, stride=CELLS), :] = f_ref[NI : NI + B, :]
    for m in range(7):
        out_ref[pl.ds(m + 1, B, stride=CELLS), :] = f_ref[B * m : B * m + B, :]

    for t in range(2):
        for copy in edge_copies(t) + tuple(ab_copies(t)):
            copy.wait_send()
    for copy in kq_copies():
        copy.wait_send()

    @pl.when(outlet)
    def _():
        for t in range(2):
            for copy in f63_copies(t):
                copy.wait_send()
        c63_copy(p + 1).wait_send()

    @pl.when(inlet)
    def _():
        for t in range(2):
            forward_copy(t).wait_send()
            f64_copy(t).wait_send()
            for copy in late_copies(t):
                copy.wait_send()


def body(pitches, field, source, couple, shift, gain, row_map, slide):
    zs = pitches // 2
    vmem = pl.BlockSpec(memory_space=pltpu.VMEM)
    dma = pltpu.SemaphoreType.DMA
    V = pltpu.VMEM
    shapes = [(B * CELLS, LINES), (B * CELLS, LINES), (B * CELLS, B), (CELLS, B), (CELLS, B)]
    shapes = [V(s, F32) for s in shapes] + [V((pitches, LINES), I32), V((1, INST), I32)]
    out = pl.pallas_call(
        functools.partial(kernel, pitches),
        out_shape=jax.ShapeDtypeStruct((B * CELLS, LINES), F32),
        in_specs=[pl.BlockSpec(memory_space=pltpu.HBM)] * 7,
        out_specs=vmem,
        scratch_shapes=shapes + [
            V((NF, LINES), F32), V((NF, LINES), F32), V((NF, LINES), F32),
            V((NI, B), F32), V((NI, B), F32),
            V((NI, NI), F32), V((NI, NI), F32), V((NI, NI), F32),
            V((4 * NR, NR), BF16), V((2 * NR, NR), BF16),
            V((NF, NI), BF16), V((NF, NI), BF16),
            V((NI, 128), BF16), V((NI, 128), BF16),
            V((128, 128), F32),
            V((NR, NR), F32), V((NR, NR), F32), V((NR, NR), F32),
            V((128, NR), BF16), V((128, NR), BF16),
            V((NR, 256), F32),
            V((NR, LINES), F32), V((B * (CHAIN + 1) + 5, LINES), F32),
            V((INST, LINES, LINES), BF16),
            V((INST, zs, 8, LINES), F32),
            V((2, 8, NF), F32), V((2, 2, 8, NF), F32),
            V((CHAIN, 40, 128), F32),
            V((2, CHAIN, 72, LINES), F32),
            V((2, 2, zs, B, LINES), F32), V((2, B, LINES), F32),
            V((2, B, LINES), F32), V((2, B, LINES), F32),
            V((B, B), F32), V((B, B), F32), V((2, B, LINES), F32),
            dma((CHAIN,)), dma((CHAIN,)), dma((2, CHAIN)), dma((2, CHAIN)),
            dma((2, 2)), dma((2, 2)), dma((2, zs)), dma((2, zs)),
            dma((2,)), dma((2,)), dma((2,)), dma((2,)), dma, dma,
            dma((2, CHAIN)), dma((2,)), dma((7,)),
        ],
        compiler_params=pltpu.CompilerParams(
            collective_id=0, has_side_effects=True, vmem_limit_bytes=60 * 2**20
        ),
        name="sweeps",
    )(
        field.transpose(1, 0, 2).reshape(B * CELLS, LINES),
        source.transpose(1, 0, 2).reshape(B * CELLS, LINES),
        couple.transpose(1, 0, 2).reshape(B * CELLS, B),
        shift, gain, row_map.reshape(pitches, LINES), slide.reshape(1, INST),
    )
    return out.reshape(B, CELLS, LINES).transpose(1, 0, 2)


def solution(mesh):
    return jax.shard_map(
        functools.partial(body, mesh.shape["pitch"]),
        mesh=mesh,
        in_specs=(
            P("axial", None, "pitch"),
            P("axial", None, "pitch"),
            P("axial", None, None),
            P("axial", None),
            P("axial", None),
            P(),
            P(),
        ),
        out_specs=P("axial", None, "pitch"),
        check_vma=False,
    )
```

```python
import functools
import math

import jax
import jax.numpy as jnp
import numpy as np
from jax import lax
from jax.experimental import pallas as pl
from jax.experimental.pallas import tpu as pltpu
from jax.sharding import PartitionSpec as P

INST, VARS, B = 7, 5, 35
CELLS, LINES, CHAIN = 8, 128, 8
NI = 256
NR = 288
NF = 384
F32, BF16, I32 = jnp.float32, jnp.bfloat16, jnp.int32
HIGHEST = lax.Precision.HIGHEST
MESH = pl.DeviceIdType.MESH

C_LOW, C_HIGH, G_LOW, G_HIGH = 0.299, 5.51, 0.00109, 0.00352
LOCAL_STEPS, REDUCED_STEPS = 7, 6
FIRST_SCALE = 0.5


def scalar_bounds(stator):
    ends = []
    for c, g in ((C_LOW, G_LOW), (C_HIGH, G_HIGH)):
        n = CELLS * CHAIN
        t = np.diag(np.full(n, 2 * c + g)) - c * np.eye(n, k=1) - c * np.eye(n, k=-1)
        if not stator:
            t[0, 0] -= c
        keep = np.arange(0, n, CELLS)
        scale = np.where(np.arange(CHAIN) == 0, FIRST_SCALE if stator else 1.0, 1.0)
        rest = np.setdiff1d(np.arange(n), keep)
        s = t[np.ix_(keep, keep)] - t[np.ix_(keep, rest)] @ np.linalg.solve(
            t[np.ix_(rest, rest)], t[np.ix_(rest, keep)]
        )
        ends.append(np.linalg.eigvalsh(scale[:, None] * s * scale[None, :]))
    return float(ends[0][0]), float(ends[1][-1])


def local_bounds():
    bend = 2 * math.cos(math.pi / CELLS)
    return C_LOW * (2 - bend) + G_LOW, C_HIGH * (2 + bend) + G_HIGH


def plan(bounds, steps):
    low, high = bounds
    mid, half = 0.5 * (high + low), 0.5 * (high - low)
    t = first = mid / half
    for _ in range(steps):
        t = 2 * t * t - 1
    return mid, half, first, 1.0 / t


def dot(a, b, precision=None, dims=((1,), (0,))):
    return lax.dot_general(a, b, (dims, ((), ())), precision=precision, preferred_element_type=F32)


def split(x):
    high = x.astype(BF16)
    return high, (x - high.astype(F32)).astype(BF16)


def dot3(a, b):
    (ah, al), (bh, bl) = a, b
    return dot(ah, bh) + (dot(ah, bl) + dot(al, bh))


def exact(a, pick, dims=((1,), (0,)), swap=False, parts=3):
    pick, total = pick.astype(BF16), None
    for _ in range(parts):
        piece = a.astype(BF16)
        a = a - piece.astype(F32)
        term = dot(pick, piece, None, dims) if swap else dot(piece, pick, None, dims)
        total = term if total is None else total + term
    return total


def iota(shape, axis):
    return lax.broadcasted_iota(I32, shape, axis)


def block_of(index, count):
    return sum(((index >= B * k).astype(I32) for k in range(1, count)), jnp.zeros_like(index))


def ones(mask):
    return jnp.where(mask, 1.0, 0.0).astype(F32)


def chebyshev(n, t, half_inv, lhs, rhs, y_ref, t_ref, steps, exact):
    eye = ones(iota((n, n), 0) == iota((n, n), 1))
    rows = 4 if exact else 3

    def load(with_y):
        th, tl = split(t_ref[...])
        lhs[0:n, 0:n] = th
        lhs[n : 2 * n, 0:n] = tl
        rhs[0:n, 0:n] = th
        rhs[n : 2 * n, 0:n] = tl
        if with_y and exact:
            lhs[2 * n : 3 * n, 0:n], lhs[3 * n : 4 * n, 0:n] = split(y_ref[...])
        elif with_y:
            lhs[2 * n : 3 * n, 0:n] = y_ref[...].astype(BF16)

    load(False)
    big = dot(lhs[0 : 2 * n, 0:n], rhs[0:n, 0:n])
    square = big[0:n] + (big[n : 2 * n] + dot(lhs[0:n, 0:n], rhs[n : 2 * n, 0:n]))
    y_ref[...] = (2.0 * half_inv) * (t * eye + t_ref[...])
    t_ref[...] = 2.0 * square - eye
    t = 2.0 * t * t - 1.0

    def step(_, t):
        load(True)
        big = dot(lhs[0 : rows * n, 0:n], rhs[0:n, 0:n])
        square = big[0:n] + (big[n : 2 * n] + dot(lhs[0:n, 0:n], rhs[n : 2 * n, 0:n]))
        mixed = big[2 * n : 3 * n]
        if exact:
            mixed += big[3 * n : 4 * n] + dot(lhs[2 * n : 3 * n, 0:n], rhs[n : 2 * n, 0:n])
        t_ref[...] = 2.0 * square - eye
        y_ref[...] = 2.0 * (t * y_ref[...] + mixed)
        return 2.0 * t * t - 1.0

    t = lax.fori_loop(0, steps - 2, step, t)
    load(True)
    big = dot(lhs[2 * n : rows * n, 0:n], rhs[0:n, 0:n])
    mixed = big[0:n]
    if exact:
        mixed += big[n : 2 * n] + dot(lhs[2 * n : 3 * n, 0:n], rhs[n : 2 * n, 0:n])
    y_ref[...] = 2.0 * (t * y_ref[...] + mixed)


def kernel(
    pitches,
    *refs,
):
    args, (out_ref, *args_v) = refs[:7], refs[7:15]
    (
        f_ref, s_ref, r_ref, g_ref, h_ref, cl_ref, cr_ref, smat, ymat, tmat, lhs, rhs, xw_h, xw_l, w_h, w_l, u_ref,
        rmat, yred, tred, yt_h, yt_l, qq, pa, pb, hot, xin,
        edge_send, edge_recv, kq, ab, corr, pass_out, pass_in, f63, f63_out, f64, f64_out, c63, c63_out, late,
        kq_s, kq_r, ab_s, ab_r, co_s, co_r, ed_s, ed_r, f63_s, f63_r, fw_s, fw_r, f64_s, f64_r, c63_s, c63_r, late_s, late_r, in_s,
    ) = refs[15:]
    field_v, source_v, couple_v, shift_v, gain_v, map_v, slide_v = args_v
    p, q = lax.axis_index("axial"), lax.axis_index("pitch")
    l = lax.rem(p, CHAIN)
    base = p - l
    stator = base > 0
    outlet, inlet = p == CHAIN - 1, p == CHAIN
    zs = pitches // 2
    core = lax.rem(q, 2)
    z = q // 2
    left, right = lax.rem(q + pitches - 1, pitches), lax.rem(q + 1, pitches)

    def at(axial, pitch):
        return {"axial": axial, "pitch": pitch}

    def remote(src, dst, send, recv, axial, pitch):
        return pltpu.make_async_remote_copy(
            src_ref=src, dst_ref=dst, send_sem=send, recv_sem=recv,
            device_id=at(axial, pitch), device_id_type=MESH,
        )

    loads = [pltpu.make_async_copy(args[i], args_v[i], in_s.at[i]) for i in range(7)]
    for load in loads:
        load.start()

    barrier = pltpu.get_barrier_semaphore()

    def greet(axial, pitch):
        pl.semaphore_signal(barrier, inc=1, device_id=at(axial, pitch), device_id_type=MESH)

    for d in range(1, CHAIN):
        greet(base + lax.rem(l + d, CHAIN), q)
    greet(p, left)
    greet(p, right)

    @pl.when(outlet)
    def _():
        greet(p + 1, q)

    @pl.when(inlet)
    def _():
        for d in range(zs):
            greet(p - 1, 2 * lax.rem(z + d, zs) + core)

    row = iota((NF, 1), 0)
    row_block = jnp.where(row < 245, block_of(row, 7), 0)
    in_sep = jnp.logical_and(row >= NI, row < NI + B)
    row_off = jnp.where(in_sep, row - NI, row - B * row_block)
    row_cell = jnp.where(row < 245, row_block + 1, jnp.where(in_sep, 0, -1))
    lane = iota((1, LINES), 1)

    def cell_of(src, i):
        return src[pl.ds(i, B, stride=CELLS), :]

    def stack(dst, src):
        dst[240:NF, :] = jnp.zeros((NF - 240, LINES), F32)
        for m in range(7):
            dst[B * m : B * m + B, :] = cell_of(src, m + 1)
        dst[NI : NI + B, :] = cell_of(src, 0)

    loads[0].wait()
    stack(f_ref, field_v)
    f63_out[0] = cell_of(field_v, CELLS - 1)
    f64_out[0] = cell_of(field_v, 0)
    loads[2].wait()
    c63_out[...] = cell_of(couple_v, CELLS - 1)

    def place_edges(t):
        pick = jnp.logical_or(
            jnp.logical_and(iota((8, LINES), 0) == 0, iota((8, LINES), 1) == 0),
            jnp.logical_and(iota((8, LINES), 0) == 1, iota((8, LINES), 1) == LINES - 1),
        )
        edge_send[t] = exact(f_ref[...], ones(pick), ((1,), (1,)), True, 2)

    place_edges(0)
    for i in (1, 3, 4, 5, 6):
        loads[i].wait()
    pl.semaphore_wait(barrier, CHAIN + 1 + jnp.where(outlet, zs, 0) + jnp.where(inlet, 1, 0))

    def edge_copies(t):
        return (
            remote(edge_send.at[t], edge_recv.at[t, 1], ed_s.at[t, 0], ed_r.at[t, 1], p, left),
            remote(edge_send.at[t], edge_recv.at[t, 0], ed_s.at[t, 1], ed_r.at[t, 0], p, right),
        )

    def f63_copies(t):
        src = f63_out.at[t]
        return [
            remote(src, f63.at[t, z], f63_s.at[t, d], f63_r.at[t, d], p + 1, 2 * lax.rem(z + d, zs) + core)
            for d in range(zs)
        ]

    def f63_arrivals(t):
        src = f63_out.at[t]
        return [
            remote(src, f63.at[t, lax.rem(z + zs - d, zs)], f63_s.at[t, d], f63_r.at[t, d], p - 1, q)
            for d in range(zs)
        ]

    def pass_copy(t):
        return remote(pass_out.at[t], pass_in.at[t], fw_s.at[t], fw_r.at[t], p, q + 1 - 2 * core)

    def f64_copy(t):
        src = f64_out.at[t]
        return remote(src, f64.at[t], f64_s.at[t], f64_r.at[t], p - 1, q)

    def f64_arrival(t):
        src = f64_out.at[t]
        return remote(src, f64.at[t], f64_s.at[t], f64_r.at[t], p + 1, q)

    def c63_copy(to):
        return remote(c63_out, c63, c63_s, c63_r, to, q)

    def kq_copies():
        return [
            remote(kq.at[l], kq.at[l], kq_s.at[d], kq_r.at[d], base + lax.rem(l + d, CHAIN), q)
            for d in range(1, CHAIN)
        ]

    def kq_arrivals():
        peers = [lax.rem(l + CHAIN - d, CHAIN) for d in range(1, CHAIN)]
        return [remote(kq.at[s], kq.at[s], kq_s.at[d + 1], kq_r.at[d + 1], base + s, q) for d, s in enumerate(peers)]

    def end_copies(t, ref, send, recv):
        return [
            remote(ref.at[t, l], ref.at[t, l], send.at[t, d], recv.at[t, d], base + lax.rem(l + d, CHAIN), q)
            for d in range(1, CHAIN)
        ]

    def end_arrivals(t, ref, send, recv):
        peers = [lax.rem(l + CHAIN - d, CHAIN) for d in range(1, CHAIN)]
        return [
            remote(ref.at[t, s], ref.at[t, s], send.at[t, d + 1], recv.at[t, d + 1], base + s, q)
            for d, s in enumerate(peers)
        ]

    ends_of, corrections = (ab, ab_s, ab_r), (corr, co_s, co_r)

    def send_inlet(t):
        @pl.when(inlet)
        def _():
            f64_copy(t).start()

    def send_outlet(t):
        @pl.when(outlet)
        def _():
            for copy in f63_copies(t):
                copy.start()

    def send_edges(t):
        for copy in edge_copies(t):
            copy.start()

    def late_copies(t):
        return [
            remote(late.at[t], late.at[t], late_s.at[t, d], late_r.at[t], base + lax.rem(l + d, CHAIN), q)
            for d in range(1, CHAIN)
        ]

    def late_arrival(t):
        return remote(late.at[t], late.at[t], late_s.at[t, 0], late_r.at[t], jnp.where(stator, CHAIN, CHAIN - 1), q)

    send_outlet(0)
    send_inlet(0)
    send_edges(0)

    @pl.when(outlet)
    def _():
        c63_copy(p + 1).start()

    stack(s_ref, source_v)
    pick_cell = ones(row_cell == iota((NF, CELLS), 1))
    own = row_off == iota((NF, B), 1)
    gain_col = jnp.sum(jnp.where(own, dot(pick_cell, gain_v[...], HIGHEST), 0.0), 1, keepdims=True)
    shift_col = jnp.sum(jnp.where(own, dot(pick_cell, shift_v[...], HIGHEST), 0.0), 1, keepdims=True)
    g_col = shift_col + 2.0 * gain_col
    place = iota((1, NF), 1)
    place_block = jnp.where(place < 245, block_of(place, 7), 0)
    place_sep = jnp.logical_and(place >= NI, place < NI + B)
    place_off = jnp.where(place_sep, place - NI, place - B * place_block)
    place_cell = jnp.where(place < 245, place_block + 1, jnp.where(place_sep, 0, -1))
    gains = dot(gain_v[...], ones(place_cell == iota((CELLS, NF), 0)), HIGHEST, ((0,), (0,)))
    gain_row = jnp.sum(jnp.where(place_off == iota((B, NF), 0), gains, 0.0), 0, keepdims=True)

    @pl.when(inlet)
    def _():
        lines = map_v[pl.ds(q, 1), :]
        xin[...] = jnp.zeros_like(xin)
        other_lines = map_v[pl.ds(q + 1 - 2 * core, 1), :]
        for whose, wanted_lines in enumerate((lines, other_lines)):
            for a in range(INST):
                found = lax.rem(wanted_lines + slide_v[:, a : a + 1], pitches * LINES)
                hot[whose, a] = ones(iota((LINES, LINES), 0) == lax.rem(found, LINES)).astype(BF16)

    cl_ref[240:NI, :] = jnp.zeros((NI - 240, B), F32)
    cr_ref[240:NI, :] = jnp.zeros((NI - 240, B), F32)
    for m in range(7):
        cl_ref[B * m : B * m + B, :] = cell_of(couple_v, m)
        cr_ref[B * m : B * m + B, :] = cell_of(couple_v, m + 1)
    col = iota((1, NI), 1)
    col_block = block_of(col, 8)
    tile = ones(iota((B, NI), 0) == col - B * col_block)
    rep_l = exact(cl_ref[...], tile)
    rep_r = exact(cr_ref[...], tile)
    in_block = block_of(iota((NI, 1), 0), 8)
    mid, half, first, scale = plan(local_bounds(), LOCAL_STEPS)
    g_in = g_col[0:NI]
    same = iota((NI, NI), 0) == iota((NI, NI), 1)
    s_full = jnp.where(in_block == col_block, rep_l + rep_r, 0.0)
    s_full -= jnp.where(col_block == in_block + 1, rep_r, 0.0)
    s_full -= jnp.where(col_block + 1 == in_block, rep_l, 0.0)
    s_full += jnp.where(same, jnp.where(iota((NI, 1), 0) < 245, g_in, mid), 0.0)
    s_full = jnp.where(jnp.logical_and(in_block == 7, jnp.logical_not(same)), 0.0, s_full)
    s_full = jnp.where(jnp.logical_and(col_block == 7, jnp.logical_not(same)), 0.0, s_full)
    smat[...] = s_full
    tmat[...] = jnp.where(same, mid - s_full, -s_full) * (1.0 / half)
    links = jnp.where(jnp.logical_and(in_block == 0, col_block == 0), rep_l, 0.0)
    links += jnp.where(jnp.logical_and(in_block == 6, col_block == 1), rep_r, 0.0)
    links = links[:, 0:128]
    links += jnp.where(iota((NI, 128), 1) == row_off[0:NI] + 2 * B, g_in, 0.0)
    chebyshev(NI, jnp.asarray(first, F32), 1.0 / half, lhs, rhs, ymat, tmat, LOCAL_STEPS, True)
    x0 = ymat[...] * scale
    ymat[...] = x0
    rest = jnp.where(same, 1.0, 0.0) - dot(smat[...], ymat[...], HIGHEST)
    inv = x0 + dot(x0.astype(BF16), rest.astype(BF16))
    xw_h[0:NI], xw_l[0:NI] = split(inv)
    w = dot3((xw_h[0:NI], xw_l[0:NI]), split(links))
    xw_h[NI:NF], xw_l[NI:NF] = split(w.T)
    w_h[...], w_l[...] = split(w)
    u_ref[...] = dot3(split(links.T), (w_h[...], w_l[...]))

    fr, to = iota((128, 128), 0), iota((128, 128), 1)
    top = ones(jnp.logical_or(
        jnp.logical_and(to < B, jnp.logical_or(fr == to + B, fr == to + 2 * B)),
        jnp.logical_and(jnp.logical_and(to >= B, to < 2 * B), fr == to),
    ))
    low = ones(jnp.logical_and(
        jnp.logical_and(to >= 2 * B, to < 3 * B), jnp.logical_or(fr == to - 2 * B, fr == to)
    ))
    sep_g = g_col[NI : NI + 40]
    part = exact(u_ref[0:40, :], top) + exact(u_ref[B : B + 40, :], low)
    part += jnp.where(iota((40, 128), 0) == iota((40, 128), 1), sep_g, 0.0)
    kq[l] = part

    @pl.when(inlet)
    def _():
        c63_copy(p - 1).wait_recv()
        kq[l, 0:B, 0:B] = kq[l, 0:B, 0:B] + c63[...]

    for copy in kq_copies():
        copy.start()

    def sides(t):
        f = f_ref[...]
        near = jnp.where(lane == 0, 0.0, pltpu.roll(f, 1, 1)) + jnp.where(
            lane == LINES - 1, 0.0, pltpu.roll(f, LINES - 1, 1)
        )
        r_ref[...] = s_ref[...] + gain_col * near
        both = dot3((xw_h[...], xw_l[...]), split(r_ref[0:NI, :]))
        ab[t, l] = (both[NI:NF] + r_ref[NI:NF, :])[0:72]
        for copy in end_copies(t, *ends_of):
            copy.start()
        r_ref[0:NI, :] = both[0:NI]

    def edges(t):
        for copy in reversed(edge_copies(t)):
            copy.wait_recv()
        ge = edge_recv[t].reshape(16, NF) * gain_row
        ge_h, ge_l = split(ge)
        short = dot3((ge_h[:, 0:NI], ge_l[:, 0:NI]), (w_h[...], w_l[...])) + ge[:, NI:NF]
        which = iota((8, 128), 0)
        corr[t, l] = jnp.where(which == 1, short[0:8], 0.0) + jnp.where(which == 0, short[8:16], 0.0)
        for copy in end_copies(t, *corrections):
            copy.start()
        spot = jnp.logical_or(
            jnp.logical_and(iota((16, LINES), 0) == 1, iota((16, LINES), 1) == 0),
            jnp.logical_and(iota((16, LINES), 0) == 8, iota((16, LINES), 1) == LINES - 1),
        )
        added = exact(ge[:, 0:NI].T, ones(spot), parts=2)
        g_ref[...] = added

    def add_edges():
        r_ref[0:NI, :] = r_ref[0:NI, :] + dot3((xw_h[0:NI], xw_l[0:NI]), split(g_ref[...]))

    def send_late(t):
        for copy in late_copies(t):
            copy.start()

    def meet_stator(t):
        f64_arrival(t).wait_recv()
        h_ref[0:208, :] = jnp.zeros((208, LINES), F32)
        h_ref[240:NI, :] = jnp.zeros((NI - 240, LINES), F32)
        h_ref[208:216, :] = jnp.zeros((8, LINES), F32)
        h_ref[210:245, :] = dot(c63_out[...], f64[t], HIGHEST)
        both = dot3((xw_h[...], xw_l[...]), split(h_ref[...]))
        late[t] = both[NI : NI + B]
        send_late(t)
        r_ref[0:NI, :] = r_ref[0:NI, :] + both[0:NI]

    def collect(t, whose, dst):
        lines = map_v[pl.ds(q if whose == 0 else q + 1 - 2 * core, 1), :]
        for a in range(INST):
            high, low_part = split(xin[a].reshape(zs * 8, LINES))
            found = lax.rem(lines + slide_v[:, a : a + 1], pitches * LINES) // LINES
            got = (dot(high, hot[whose, a]) + dot(low_part, hot[whose, a])).reshape(zs, 8, LINES)
            which = 2 * iota((zs, 1, LINES), 0) + core == found.reshape(1, 1, LINES)
            dst[VARS * a : VARS * a + VARS, :] = jnp.sum(jnp.where(which, got, 0.0), 0)[0:VARS]

    def meet_rotor(t):
        for copy in f63_arrivals(t):
            copy.wait_recv()
        for a in range(INST):
            xin[a, :, 0:VARS, :] = f63[t, :, VARS * a : VARS * a + VARS, :]
        collect(t, 1, pass_out.at[t])
        pass_copy(t).start()
        collect(t, 0, u_ref)
        pass_copy(t).wait_recv()
        late[t] = dot(c63[...], u_ref[0:B, :] + pass_in[t], HIGHEST)
        send_late(t)

    def interface(t):
        @pl.when(outlet)
        def _():
            meet_stator(t)

        @pl.when(inlet)
        def _():
            meet_rotor(t)

    def finish(t):
        for copy in end_arrivals(t, *ends_of) + end_arrivals(t, *corrections):
            copy.wait_recv()
        spread = exact(corr[t].reshape(8 * CHAIN, 128).T, spread_pick, parts=2)
        for s in range(CHAIN):
            piece = spread[:, LINES * s : LINES * s + LINES]
            pa[B * s : B * s + B, :] = ab[t, s, 0:B, :] + piece[0:B]
            pb[B * s + B : B * s + 2 * B, :] = ab[t, s, B : 2 * B, :] + piece[B : 2 * B]

        @pl.when(jnp.logical_not(jnp.logical_or(inlet, outlet)))
        def _():
            late_arrival(t).wait_recv()

        @pl.when(stator)
        def _():
            pa[0:B, :] = pa[0:B, :] + late[t]

        @pl.when(jnp.logical_not(stator))
        def _():
            pa[B * (CHAIN - 1) : B * CHAIN, :] = pa[B * (CHAIN - 1) : B * CHAIN, :] + late[t]

        ends = dot3((yt_h[...], yt_l[...]), split(pa[...] + pb[0:NR, :]))
        if t == 0:
            f64_out[1] = ends[0:B]
            send_inlet(1)
        f_ref[0:NI, :] = r_ref[0:NI, :] + dot3((w_h[...], w_l[...]), split(ends))
        f_ref[NI:NF, :] = ends

    sides(0)
    edges(0)
    add_edges()
    interface(0)
    pb[0:B, :] = jnp.zeros((B, LINES), F32)
    pa[B * CHAIN : NR, :] = jnp.zeros((NR - B * CHAIN, LINES), F32)
    lines_at, pick_at = iota((8 * CHAIN, LINES * CHAIN), 1), iota((8 * CHAIN, LINES * CHAIN), 0)
    spread_pick = ones(jnp.logical_or(
        lines_at == LINES * (pick_at // 8) + jnp.where(lax.rem(pick_at, 8) == 1, 0, -1 - LINES * CHAIN),
        lines_at == LINES * (pick_at // 8) + jnp.where(lax.rem(pick_at, 8) == 0, LINES - 1, -1 - LINES * CHAIN),
    )).astype(BF16)

    for copy in kq_arrivals():
        copy.wait_recv()
    qq[0:B, 128:256] = jnp.zeros((B, 128), F32)
    qq[B * CHAIN : NR, :] = jnp.zeros((NR - B * CHAIN, 256), F32)
    for s in range(CHAIN):
        qq[B * s : B * s + B, 0:128] = kq[s, 0:B, :]
        if s + 1 < CHAIN:
            qq[B * s + B : B * s + 2 * B, 128:256] = kq[s, 0:B, :]
    rcol, rrow = iota((1, NR), 1), iota((NR, 1), 0)
    rcol_block, rrow_block = block_of(rcol, 9), block_of(rrow, 9)
    rcol_off, rrow_off = rcol - B * rcol_block, rrow - B * rrow_block
    source_row = iota((256, NR), 0)
    diag_tile = ones(jnp.logical_or(source_row == rcol_off, source_row == rcol_off + 128 + 2 * B))
    link_tile = ones(iota((128, NR), 0) == rcol_off + B)
    link_turn = ones(iota((NR, 128), 1) == rrow_off + B)
    diag = exact(qq[...], diag_tile)
    above = exact(qq[:, 0:128], link_tile)
    below = exact(qq[:, 0:128], link_turn, ((1,), (1,)), True)
    rotor_plan, stator_plan = plan(scalar_bounds(False), REDUCED_STEPS), plan(scalar_bounds(True), REDUCED_STEPS)
    mid, half_inv, first, scale = (
        jnp.where(stator, jnp.asarray(b, F32), jnp.asarray(a, F32))
        for a, b in zip(
            (rotor_plan[0], 1.0 / rotor_plan[1], rotor_plan[2], rotor_plan[3]),
            (stator_plan[0], 1.0 / stator_plan[1], stator_plan[2], stator_plan[3]),
        )
    )
    same = iota((NR, NR), 0) == iota((NR, NR), 1)
    live = jnp.logical_and(rrow_block < CHAIN, rcol_block < CHAIN)
    red = jnp.where(rcol_block == rrow_block, diag, 0.0)
    red -= jnp.where(rcol_block == rrow_block + 1, above, 0.0)
    red -= jnp.where(rcol_block + 1 == rrow_block, below, 0.0)
    first_scale = jnp.where(stator, jnp.asarray(FIRST_SCALE, F32), jnp.asarray(1.0, F32))
    row_scale, col_scale = (jnp.where(i < B, first_scale, 1.0) for i in (rrow, rcol))
    red = jnp.where(live, red * (row_scale * col_scale), jnp.where(same, mid, 0.0))
    rmat[...] = red
    tred[...] = jnp.where(same, mid - red, -red) * half_inv
    chebyshev(NR, first, half_inv, lhs, rhs, yred, tred, REDUCED_STEPS, False)
    xr = yred[...] * scale
    want = jnp.logical_and(
        jnp.logical_and(iota((128, NR), 1) == iota((128, NR), 0) + B * l, iota((128, NR), 0) < 2 * B),
        iota((128, NR), 1) < B * CHAIN,
    )
    wanted = jnp.where(want, col_scale, 0.0)
    yred[...] = xr
    few = wanted[0:80]
    y = dot3(split(few), split(yred[...]))
    y += dot((few - dot3(split(y), split(rmat[...]))).astype(BF16), yred[...].astype(BF16))
    y += dot((few - dot(y, rmat[...], HIGHEST)).astype(BF16), yred[...].astype(BF16))
    yt_h[80:128], yt_l[80:128] = jnp.zeros((48, NR), BF16), jnp.zeros((48, NR), BF16)
    yt_h[0:80], yt_l[0:80] = split(y * col_scale)

    finish(0)

    f63_out[1] = f_ref[210:245, :]
    send_outlet(1)
    place_edges(1)
    send_edges(1)
    sides(1)
    edges(1)
    interface(1)
    add_edges()
    finish(1)
    out_ref[pl.ds(0, B, stride=CELLS), :] = f_ref[NI : NI + B, :]
    for m in range(7):
        out_ref[pl.ds(m + 1, B, stride=CELLS), :] = f_ref[B * m : B * m + B, :]

    for t in range(2):
        for copy in list(edge_copies(t)) + end_copies(t, *ends_of) + end_copies(t, *corrections):
            copy.wait_send()
    for copy in kq_copies():
        copy.wait_send()

    @pl.when(outlet)
    def _():
        for t in range(2):
            for copy in f63_copies(t) + late_copies(t):
                copy.wait_send()
        c63_copy(p + 1).wait_send()

    @pl.when(inlet)
    def _():
        for t in range(2):
            pass_copy(t).wait_send()
            f64_copy(t).wait_send()
            for copy in late_copies(t):
                copy.wait_send()


def body(pitches, field, source, couple, shift, gain, row_map, slide):
    zs = pitches // 2
    vmem = pl.BlockSpec(memory_space=pltpu.VMEM)
    dma = pltpu.SemaphoreType.DMA
    V = pltpu.VMEM
    shapes = [(B * CELLS, LINES), (B * CELLS, LINES), (B * CELLS, B), (CELLS, B), (CELLS, B)]
    shapes = [V(s, F32) for s in shapes] + [V((pitches, LINES), I32), V((1, INST), I32)]
    out = pl.pallas_call(
        functools.partial(kernel, pitches),
        out_shape=jax.ShapeDtypeStruct((B * CELLS, LINES), F32),
        in_specs=[pl.BlockSpec(memory_space=pltpu.HBM)] * 7,
        out_specs=vmem,
        scratch_shapes=shapes + [
            V((NF, LINES), F32), V((NF, LINES), F32), V((NF, LINES), F32),
            V((NI, LINES), F32), V((NI, LINES), F32),
            V((NI, B), F32), V((NI, B), F32),
            V((NI, NI), F32), V((NI, NI), F32), V((NI, NI), F32),
            V((4 * NR, NR), BF16), V((2 * NR, NR), BF16),
            V((NF, NI), BF16), V((NF, NI), BF16),
            V((NI, 128), BF16), V((NI, 128), BF16),
            V((128, 128), F32),
            V((NR, NR), F32), V((NR, NR), F32), V((NR, NR), F32),
            V((128, NR), BF16), V((128, NR), BF16),
            V((NR, 256), F32),
            V((NR, LINES), F32), V((B * (CHAIN + 1) + 5, LINES), F32),
            V((2, INST, LINES, LINES), BF16),
            V((INST, zs, 8, LINES), F32),
            V((2, 8, NF), F32), V((2, 2, 8, NF), F32),
            V((CHAIN, 40, 128), F32),
            V((2, CHAIN, 72, LINES), F32), V((2, CHAIN, 8, 128), F32),
            V((2, B, LINES), F32), V((2, B, LINES), F32),
            V((2, zs, B, LINES), F32), V((2, B, LINES), F32),
            V((2, B, LINES), F32), V((2, B, LINES), F32),
            V((B, B), F32), V((B, B), F32), V((2, B, LINES), F32),
            dma((CHAIN,)), dma((CHAIN,)), dma((2, CHAIN)), dma((2, CHAIN)), dma((2, CHAIN)), dma((2, CHAIN)),
            dma((2, 2)), dma((2, 2)), dma((2, zs)), dma((2, zs)),
            dma((2,)), dma((2,)), dma((2,)), dma((2,)), dma, dma,
            dma((2, CHAIN)), dma((2,)), dma((7,)),
        ],
        compiler_params=pltpu.CompilerParams(
            collective_id=0, has_side_effects=True, vmem_limit_bytes=60 * 2**20
        ),
        name="sweeps",
    )(
        field.transpose(1, 0, 2).reshape(B * CELLS, LINES),
        source.transpose(1, 0, 2).reshape(B * CELLS, LINES),
        couple.transpose(1, 0, 2).reshape(B * CELLS, B),
        shift, gain, row_map.reshape(pitches, LINES), slide.reshape(1, INST),
    )
    return out.reshape(B, CELLS, LINES).transpose(1, 0, 2)


def solution(mesh):
    return jax.shard_map(
        functools.partial(body, mesh.shape["pitch"]),
        mesh=mesh,
        in_specs=(
            P("axial", None, "pitch"),
            P("axial", None, "pitch"),
            P("axial", None, None),
            P("axial", None),
            P("axial", None),
            P(),
            P(),
        ),
        out_specs=P("axial", None, "pitch"),
        check_vma=False,
    )
```

```python
import functools
import math

import jax
import jax.numpy as jnp
import numpy as np
from jax import lax
from jax.experimental import pallas as pl
from jax.experimental.pallas import tpu as pltpu
from jax.sharding import PartitionSpec as P

INST, VARS, B = 7, 5, 35
CELLS, LINES, CHAIN = 8, 128, 8
NI = 256
NR = 288
NF = 384
F32, BF16, I32 = jnp.float32, jnp.bfloat16, jnp.int32
HIGHEST = lax.Precision.HIGHEST
MESH = pl.DeviceIdType.MESH

C_LOW, C_HIGH, G_LOW, G_HIGH = 0.299, 5.51, 0.00109, 0.00352
LOCAL_STEPS, REDUCED_STEPS = 7, 6
FIRST_SCALE = 0.5


def scalar_bounds(stator):
    ends = []
    for c, g in ((C_LOW, G_LOW), (C_HIGH, G_HIGH)):
        n = CELLS * CHAIN
        t = np.diag(np.full(n, 2 * c + g)) - c * np.eye(n, k=1) - c * np.eye(n, k=-1)
        if not stator:
            t[0, 0] -= c
        keep = np.arange(0, n, CELLS)
        scale = np.where(np.arange(CHAIN) == 0, FIRST_SCALE if stator else 1.0, 1.0)
        rest = np.setdiff1d(np.arange(n), keep)
        s = t[np.ix_(keep, keep)] - t[np.ix_(keep, rest)] @ np.linalg.solve(
            t[np.ix_(rest, rest)], t[np.ix_(rest, keep)]
        )
        ends.append(np.linalg.eigvalsh(scale[:, None] * s * scale[None, :]))
    return float(ends[0][0]), float(ends[1][-1])


def local_bounds():
    bend = 2 * math.cos(math.pi / CELLS)
    return C_LOW * (2 - bend) + G_LOW, C_HIGH * (2 + bend) + G_HIGH


def plan(bounds, steps):
    low, high = bounds
    mid, half = 0.5 * (high + low), 0.5 * (high - low)
    t = first = mid / half
    for _ in range(steps):
        t = 2 * t * t - 1
    return mid, half, first, 1.0 / t


def dot(a, b, precision=None, dims=((1,), (0,))):
    return lax.dot_general(a, b, (dims, ((), ())), precision=precision, preferred_element_type=F32)


def split(x):
    high = x.astype(BF16)
    return high, (x - high.astype(F32)).astype(BF16)


def dot3(a, b):
    (ah, al), (bh, bl) = a, b
    return dot(ah, bh) + (dot(ah, bl) + dot(al, bh))


def exact(a, pick, dims=((1,), (0,)), swap=False, parts=3):
    pick, total = pick.astype(BF16), None
    for _ in range(parts):
        piece = a.astype(BF16)
        a = a - piece.astype(F32)
        term = dot(pick, piece, None, dims) if swap else dot(piece, pick, None, dims)
        total = term if total is None else total + term
    return total


def iota(shape, axis):
    return lax.broadcasted_iota(I32, shape, axis)


def block_of(index, count):
    return sum(((index >= B * k).astype(I32) for k in range(1, count)), jnp.zeros_like(index))


def ones(mask):
    return jnp.where(mask, 1.0, 0.0).astype(F32)


def chebyshev(n, t, half_inv, lhs, rhs, y_ref, t_ref, steps, exact):
    eye = ones(iota((n, n), 0) == iota((n, n), 1))
    rows = 4 if exact else 3

    def load(with_y):
        th, tl = split(t_ref[...])
        lhs[0:n, 0:n] = th
        lhs[n : 2 * n, 0:n] = tl
        rhs[0:n, 0:n] = th
        rhs[n : 2 * n, 0:n] = tl
        if with_y and exact:
            lhs[2 * n : 3 * n, 0:n], lhs[3 * n : 4 * n, 0:n] = split(y_ref[...])
        elif with_y:
            lhs[2 * n : 3 * n, 0:n] = y_ref[...].astype(BF16)

    load(False)
    big = dot(lhs[0 : 2 * n, 0:n], rhs[0:n, 0:n])
    square = big[0:n] + (big[n : 2 * n] + dot(lhs[0:n, 0:n], rhs[n : 2 * n, 0:n]))
    y_ref[...] = (2.0 * half_inv) * (t * eye + t_ref[...])
    t_ref[...] = 2.0 * square - eye
    t = 2.0 * t * t - 1.0

    def step(_, t):
        load(True)
        big = dot(lhs[0 : rows * n, 0:n], rhs[0:n, 0:n])
        square = big[0:n] + (big[n : 2 * n] + dot(lhs[0:n, 0:n], rhs[n : 2 * n, 0:n]))
        mixed = big[2 * n : 3 * n]
        if exact:
            mixed += big[3 * n : 4 * n] + dot(lhs[2 * n : 3 * n, 0:n], rhs[n : 2 * n, 0:n])
        t_ref[...] = 2.0 * square - eye
        y_ref[...] = 2.0 * (t * y_ref[...] + mixed)
        return 2.0 * t * t - 1.0

    t = lax.fori_loop(0, steps - 2, step, t)
    load(True)
    big = dot(lhs[2 * n : rows * n, 0:n], rhs[0:n, 0:n])
    mixed = big[0:n]
    if exact:
        mixed += big[n : 2 * n] + dot(lhs[2 * n : 3 * n, 0:n], rhs[n : 2 * n, 0:n])
    y_ref[...] = 2.0 * (t * y_ref[...] + mixed)


def kernel(
    pitches,
    *refs,
):
    args, (out_ref, *args_v) = refs[:7], refs[7:15]
    (
        f_ref, s_ref, r_ref, g_ref, h_ref, cl_ref, cr_ref, smat, ymat, tmat, lhs, rhs, xw_h, xw_l, w_h, w_l, u_ref,
        rmat, yred, tred, yt_h, yt_l, qq, pa, pb, hot, xin,
        edge_send, edge_recv, kq, ab, corr, pass_out, pass_in, f63, f63_out, f64, f64_out, c63, c63_out, late,
        kq_s, kq_r, ab_s, ab_r, co_s, co_r, ed_s, ed_r, f63_s, f63_r, fw_s, fw_r, f64_s, f64_r, c63_s, c63_r, late_s, late_r, in_s,
    ) = refs[15:]
    field_v, source_v, couple_v, shift_v, gain_v, map_v, slide_v = args_v
    p, q = lax.axis_index("axial"), lax.axis_index("pitch")
    l = lax.rem(p, CHAIN)
    base = p - l
    stator = base > 0
    outlet, inlet = p == CHAIN - 1, p == CHAIN
    zs = pitches // 2
    core = lax.rem(q, 2)
    z = q // 2
    left, right = lax.rem(q + pitches - 1, pitches), lax.rem(q + 1, pitches)

    def at(axial, pitch):
        return {"axial": axial, "pitch": pitch}

    def remote(src, dst, send, recv, axial, pitch):
        return pltpu.make_async_remote_copy(
            src_ref=src, dst_ref=dst, send_sem=send, recv_sem=recv,
            device_id=at(axial, pitch), device_id_type=MESH,
        )

    loads = [pltpu.make_async_copy(args[i], args_v[i], in_s.at[i]) for i in range(7)]
    for load in loads:
        load.start()

    barrier = pltpu.get_barrier_semaphore()

    def greet(axial, pitch):
        pl.semaphore_signal(barrier, inc=1, device_id=at(axial, pitch), device_id_type=MESH)

    for d in range(1, CHAIN):
        greet(base + lax.rem(l + d, CHAIN), q)
    greet(p, left)
    greet(p, right)

    @pl.when(outlet)
    def _():
        greet(p + 1, q)

    @pl.when(inlet)
    def _():
        for d in range(zs):
            greet(p - 1, 2 * lax.rem(z + d, zs) + core)

    row = iota((NF, 1), 0)
    row_block = jnp.where(row < 245, block_of(row, 7), 0)
    in_sep = jnp.logical_and(row >= NI, row < NI + B)
    row_off = jnp.where(in_sep, row - NI, row - B * row_block)
    row_cell = jnp.where(row < 245, row_block + 1, jnp.where(in_sep, 0, -1))
    lane = iota((1, LINES), 1)

    def cell_of(src, i):
        return src[pl.ds(i, B, stride=CELLS), :]

    def stack(dst, src):
        dst[240:NF, :] = jnp.zeros((NF - 240, LINES), F32)
        for m in range(7):
            dst[B * m : B * m + B, :] = cell_of(src, m + 1)
        dst[NI : NI + B, :] = cell_of(src, 0)

    loads[0].wait()
    stack(f_ref, field_v)
    f63_out[0] = cell_of(field_v, CELLS - 1)
    f64_out[0] = cell_of(field_v, 0)
    loads[2].wait()
    c63_out[...] = cell_of(couple_v, CELLS - 1)

    def place_edges(t):
        pick = jnp.logical_or(
            jnp.logical_and(iota((8, LINES), 0) == 0, iota((8, LINES), 1) == 0),
            jnp.logical_and(iota((8, LINES), 0) == 1, iota((8, LINES), 1) == LINES - 1),
        )
        edge_send[t] = exact(f_ref[...], ones(pick), ((1,), (1,)), True, 2)

    place_edges(0)
    for i in (1, 3, 4, 5, 6):
        loads[i].wait()

    def edge_copies(t):
        return (
            remote(edge_send.at[t], edge_recv.at[t, 1], ed_s.at[t, 0], ed_r.at[t, 1], p, left),
            remote(edge_send.at[t], edge_recv.at[t, 0], ed_s.at[t, 1], ed_r.at[t, 0], p, right),
        )

    def f63_copies(t):
        src = f63_out.at[t]
        return [
            remote(src, f63.at[t, z], f63_s.at[t, d], f63_r.at[t, d], p + 1, 2 * lax.rem(z + d, zs) + core)
            for d in range(zs)
        ]

    def f63_arrivals(t):
        src = f63_out.at[t]
        return [
            remote(src, f63.at[t, lax.rem(z + zs - d, zs)], f63_s.at[t, d], f63_r.at[t, d], p - 1, q)
            for d in range(zs)
        ]

    def pass_copy(t):
        return remote(pass_out.at[t], pass_in.at[t], fw_s.at[t], fw_r.at[t], p, q + 1 - 2 * core)

    def f64_copy(t):
        src = f64_out.at[t]
        return remote(src, f64.at[t], f64_s.at[t], f64_r.at[t], p - 1, q)

    def f64_arrival(t):
        src = f64_out.at[t]
        return remote(src, f64.at[t], f64_s.at[t], f64_r.at[t], p + 1, q)

    def c63_copy(to):
        return remote(c63_out, c63, c63_s, c63_r, to, q)

    def kq_copies():
        return [
            remote(kq.at[l], kq.at[l], kq_s.at[d], kq_r.at[d], base + lax.rem(l + d, CHAIN), q)
            for d in range(1, CHAIN)
        ]

    def kq_arrivals():
        peers = [lax.rem(l + CHAIN - d, CHAIN) for d in range(1, CHAIN)]
        return [remote(kq.at[s], kq.at[s], kq_s.at[d + 1], kq_r.at[d + 1], base + s, q) for d, s in enumerate(peers)]

    def end_copies(t, ref, send, recv):
        return [
            remote(ref.at[t, l], ref.at[t, l], send.at[t, d], recv.at[t, d], base + lax.rem(l + d, CHAIN), q)
            for d in range(1, CHAIN)
        ]

    def end_arrivals(t, ref, send, recv):
        peers = [lax.rem(l + CHAIN - d, CHAIN) for d in range(1, CHAIN)]
        return [
            remote(ref.at[t, s], ref.at[t, s], send.at[t, d + 1], recv.at[t, d + 1], base + s, q)
            for d, s in enumerate(peers)
        ]

    ends_of, corrections = (ab, ab_s, ab_r), (corr, co_s, co_r)

    def send_inlet(t):
        @pl.when(inlet)
        def _():
            f64_copy(t).start()

    def send_outlet(t):
        @pl.when(outlet)
        def _():
            for copy in f63_copies(t):
                copy.start()

    def send_edges(t):
        for copy in edge_copies(t):
            copy.start()

    def late_copies(t):
        return [
            remote(late.at[t], late.at[t], late_s.at[t, d], late_r.at[t], base + lax.rem(l + d, CHAIN), q)
            for d in range(1, CHAIN)
        ]

    def late_arrival(t):
        return remote(late.at[t], late.at[t], late_s.at[t, 0], late_r.at[t], jnp.where(stator, CHAIN, CHAIN - 1), q)

    stack(s_ref, source_v)
    pick_cell = ones(row_cell == iota((NF, CELLS), 1))
    own = row_off == iota((NF, B), 1)
    gain_col = jnp.sum(jnp.where(own, dot(pick_cell, gain_v[...], HIGHEST), 0.0), 1, keepdims=True)
    shift_col = jnp.sum(jnp.where(own, dot(pick_cell, shift_v[...], HIGHEST), 0.0), 1, keepdims=True)
    g_col = shift_col + 2.0 * gain_col
    place = iota((1, NF), 1)
    place_block = jnp.where(place < 245, block_of(place, 7), 0)
    place_sep = jnp.logical_and(place >= NI, place < NI + B)
    place_off = jnp.where(place_sep, place - NI, place - B * place_block)
    place_cell = jnp.where(place < 245, place_block + 1, jnp.where(place_sep, 0, -1))
    gains = dot(gain_v[...], ones(place_cell == iota((CELLS, NF), 0)), HIGHEST, ((0,), (0,)))
    gain_row = jnp.sum(jnp.where(place_off == iota((B, NF), 0), gains, 0.0), 0, keepdims=True)

    @pl.when(inlet)
    def _():
        lines = map_v[pl.ds(q, 1), :]
        xin[...] = jnp.zeros_like(xin)
        other_lines = map_v[pl.ds(q + 1 - 2 * core, 1), :]
        for whose, wanted_lines in enumerate((lines, other_lines)):
            for a in range(INST):
                found = lax.rem(wanted_lines + slide_v[:, a : a + 1], pitches * LINES)
                hot[whose, a] = ones(iota((LINES, LINES), 0) == lax.rem(found, LINES)).astype(BF16)

    cl_ref[240:NI, :] = jnp.zeros((NI - 240, B), F32)
    cr_ref[240:NI, :] = jnp.zeros((NI - 240, B), F32)
    for m in range(7):
        cl_ref[B * m : B * m + B, :] = cell_of(couple_v, m)
        cr_ref[B * m : B * m + B, :] = cell_of(couple_v, m + 1)
    col = iota((1, NI), 1)
    col_block = block_of(col, 8)
    tile = ones(iota((B, NI), 0) == col - B * col_block)
    rep_l = exact(cl_ref[...], tile)
    rep_r = exact(cr_ref[...], tile)
    in_block = block_of(iota((NI, 1), 0), 8)
    mid, half, first, scale = plan(local_bounds(), LOCAL_STEPS)
    g_in = g_col[0:NI]
    same = iota((NI, NI), 0) == iota((NI, NI), 1)
    s_full = jnp.where(in_block == col_block, rep_l + rep_r, 0.0)
    s_full -= jnp.where(col_block == in_block + 1, rep_r, 0.0)
    s_full -= jnp.where(col_block + 1 == in_block, rep_l, 0.0)
    s_full += jnp.where(same, jnp.where(iota((NI, 1), 0) < 245, g_in, mid), 0.0)
    s_full = jnp.where(jnp.logical_and(in_block == 7, jnp.logical_not(same)), 0.0, s_full)
    s_full = jnp.where(jnp.logical_and(col_block == 7, jnp.logical_not(same)), 0.0, s_full)
    smat[...] = s_full
    tmat[...] = jnp.where(same, mid - s_full, -s_full) * (1.0 / half)
    links = jnp.where(jnp.logical_and(in_block == 0, col_block == 0), rep_l, 0.0)
    links += jnp.where(jnp.logical_and(in_block == 6, col_block == 1), rep_r, 0.0)
    links = links[:, 0:128]
    links += jnp.where(iota((NI, 128), 1) == row_off[0:NI] + 2 * B, g_in, 0.0)
    chebyshev(NI, jnp.asarray(first, F32), 1.0 / half, lhs, rhs, ymat, tmat, LOCAL_STEPS, True)
    pl.semaphore_wait(barrier, CHAIN + 1 + jnp.where(outlet, zs, 0) + jnp.where(inlet, 1, 0))
    send_outlet(0)
    send_inlet(0)
    send_edges(0)

    @pl.when(outlet)
    def _():
        c63_copy(p + 1).start()

    x0 = ymat[...] * scale
    ymat[...] = x0
    rest = jnp.where(same, 1.0, 0.0) - dot(smat[...], ymat[...], HIGHEST)
    inv = x0 + dot(x0.astype(BF16), rest.astype(BF16))
    xw_h[0:NI], xw_l[0:NI] = split(inv)
    w = dot3((xw_h[0:NI], xw_l[0:NI]), split(links))
    xw_h[NI:NF], xw_l[NI:NF] = split(w.T)
    w_h[...], w_l[...] = split(w)
    u_ref[...] = dot3(split(links.T), (w_h[...], w_l[...]))

    fr, to = iota((128, 128), 0), iota((128, 128), 1)
    top = ones(jnp.logical_or(
        jnp.logical_and(to < B, jnp.logical_or(fr == to + B, fr == to + 2 * B)),
        jnp.logical_and(jnp.logical_and(to >= B, to < 2 * B), fr == to),
    ))
    low = ones(jnp.logical_and(
        jnp.logical_and(to >= 2 * B, to < 3 * B), jnp.logical_or(fr == to - 2 * B, fr == to)
    ))
    sep_g = g_col[NI : NI + 40]
    part = exact(u_ref[0:40, :], top) + exact(u_ref[B : B + 40, :], low)
    part += jnp.where(iota((40, 128), 0) == iota((40, 128), 1), sep_g, 0.0)
    kq[l] = part

    @pl.when(inlet)
    def _():
        c63_copy(p - 1).wait_recv()
        kq[l, 0:B, 0:B] = kq[l, 0:B, 0:B] + c63[...]

    for copy in kq_copies():
        copy.start()

    def send_ends(t):
        for copy in end_copies(t, *ends_of):
            copy.start()

    def send_corrections(t):
        for copy in end_copies(t, *corrections):
            copy.start()

    def sides(t):
        f = f_ref[...]
        near = jnp.where(lane == 0, 0.0, pltpu.roll(f, 1, 1)) + jnp.where(
            lane == LINES - 1, 0.0, pltpu.roll(f, LINES - 1, 1)
        )
        r_ref[...] = s_ref[...] + gain_col * near
        both = dot3((xw_h[...], xw_l[...]), split(r_ref[0:NI, :]))
        ab[t, l] = (both[NI:NF] + r_ref[NI:NF, :])[0:72]
        if t == 1:
            send_ends(t)
        r_ref[0:NI, :] = both[0:NI]

    def edges(t):
        for copy in reversed(edge_copies(t)):
            copy.wait_recv()
        ge = edge_recv[t].reshape(16, NF) * gain_row
        ge_h, ge_l = split(ge)
        short = dot3((ge_h[:, 0:NI], ge_l[:, 0:NI]), (w_h[...], w_l[...])) + ge[:, NI:NF]
        which = iota((8, 128), 0)
        corr[t, l] = jnp.where(which == 1, short[0:8], 0.0) + jnp.where(which == 0, short[8:16], 0.0)
        if t == 1:
            send_corrections(t)
        spot = jnp.logical_or(
            jnp.logical_and(iota((16, LINES), 0) == 1, iota((16, LINES), 1) == 0),
            jnp.logical_and(iota((16, LINES), 0) == 8, iota((16, LINES), 1) == LINES - 1),
        )
        added = exact(ge[:, 0:NI].T, ones(spot), parts=2)
        g_ref[...] = added

    def add_edges():
        r_ref[0:NI, :] = r_ref[0:NI, :] + dot3((xw_h[0:NI], xw_l[0:NI]), split(g_ref[...]))

    def send_late(t):
        for copy in late_copies(t):
            copy.start()

    def meet_stator(t):
        f64_arrival(t).wait_recv()
        h_ref[0:208, :] = jnp.zeros((208, LINES), F32)
        h_ref[240:NI, :] = jnp.zeros((NI - 240, LINES), F32)
        h_ref[208:216, :] = jnp.zeros((8, LINES), F32)
        h_ref[210:245, :] = dot(c63_out[...], f64[t], HIGHEST)
        both = dot3((xw_h[...], xw_l[...]), split(h_ref[...]))
        late[t] = both[NI : NI + B]
        send_late(t)
        r_ref[0:NI, :] = r_ref[0:NI, :] + both[0:NI]

    def collect(t, whose, dst):
        lines = map_v[pl.ds(q if whose == 0 else q + 1 - 2 * core, 1), :]
        for a in range(INST):
            high, low_part = split(xin[a].reshape(zs * 8, LINES))
            found = lax.rem(lines + slide_v[:, a : a + 1], pitches * LINES) // LINES
            got = (dot(high, hot[whose, a]) + dot(low_part, hot[whose, a])).reshape(zs, 8, LINES)
            which = 2 * iota((zs, 1, LINES), 0) + core == found.reshape(1, 1, LINES)
            dst[VARS * a : VARS * a + VARS, :] = jnp.sum(jnp.where(which, got, 0.0), 0)[0:VARS]

    def meet_rotor(t):
        for copy in f63_arrivals(t):
            copy.wait_recv()
        for a in range(INST):
            xin[a, :, 0:VARS, :] = f63[t, :, VARS * a : VARS * a + VARS, :]
        collect(t, 1, pass_out.at[t])
        pass_copy(t).start()
        collect(t, 0, u_ref)
        pass_copy(t).wait_recv()
        late[t] = dot(c63[...], u_ref[0:B, :] + pass_in[t], HIGHEST)
        send_late(t)

    def interface(t):
        @pl.when(outlet)
        def _():
            meet_stator(t)

        @pl.when(inlet)
        def _():
            meet_rotor(t)

    def finish(t):
        for copy in end_arrivals(t, *ends_of) + end_arrivals(t, *corrections):
            copy.wait_recv()
        spread = exact(corr[t].reshape(8 * CHAIN, 128).T, spread_pick, parts=2)
        for s in range(CHAIN):
            piece = spread[:, LINES * s : LINES * s + LINES]
            pa[B * s : B * s + B, :] = ab[t, s, 0:B, :] + piece[0:B]
            pb[B * s + B : B * s + 2 * B, :] = ab[t, s, B : 2 * B, :] + piece[B : 2 * B]

        @pl.when(jnp.logical_not(jnp.logical_or(inlet, outlet)))
        def _():
            late_arrival(t).wait_recv()

        @pl.when(stator)
        def _():
            pa[0:B, :] = pa[0:B, :] + late[t]

        @pl.when(jnp.logical_not(stator))
        def _():
            pa[B * (CHAIN - 1) : B * CHAIN, :] = pa[B * (CHAIN - 1) : B * CHAIN, :] + late[t]

        ends = dot3((yt_h[...], yt_l[...]), split(pa[...] + pb[0:NR, :]))
        if t == 0:
            f64_out[1] = ends[0:B]
            send_inlet(1)

            @pl.when(outlet)
            def _():
                h_ref[208:NI, :] = r_ref[208:NI, :] + dot3((w_h[208:NI], w_l[208:NI]), split(ends))
                f63_out[1] = h_ref[210:245, :]

            send_outlet(1)
        f_ref[0:NI, :] = r_ref[0:NI, :] + dot3((w_h[...], w_l[...]), split(ends))
        f_ref[NI:NF, :] = ends

    sides(0)
    edges(0)
    add_edges()
    pb[0:B, :] = jnp.zeros((B, LINES), F32)
    pa[B * CHAIN : NR, :] = jnp.zeros((NR - B * CHAIN, LINES), F32)
    lines_at, pick_at = iota((8 * CHAIN, LINES * CHAIN), 1), iota((8 * CHAIN, LINES * CHAIN), 0)
    spread_pick = ones(jnp.logical_or(
        lines_at == LINES * (pick_at // 8) + jnp.where(lax.rem(pick_at, 8) == 1, 0, -1 - LINES * CHAIN),
        lines_at == LINES * (pick_at // 8) + jnp.where(lax.rem(pick_at, 8) == 0, LINES - 1, -1 - LINES * CHAIN),
    )).astype(BF16)

    for copy in kq_arrivals():
        copy.wait_recv()
    send_ends(0)
    send_corrections(0)
    interface(0)
    qq[0:B, 128:256] = jnp.zeros((B, 128), F32)
    qq[B * CHAIN : NR, :] = jnp.zeros((NR - B * CHAIN, 256), F32)
    for s in range(CHAIN):
        qq[B * s : B * s + B, 0:128] = kq[s, 0:B, :]
        if s + 1 < CHAIN:
            qq[B * s + B : B * s + 2 * B, 128:256] = kq[s, 0:B, :]
    rcol, rrow = iota((1, NR), 1), iota((NR, 1), 0)
    rcol_block, rrow_block = block_of(rcol, 9), block_of(rrow, 9)
    rcol_off, rrow_off = rcol - B * rcol_block, rrow - B * rrow_block
    source_row = iota((256, NR), 0)
    diag_tile = ones(jnp.logical_or(source_row == rcol_off, source_row == rcol_off + 128 + 2 * B))
    link_tile = ones(iota((128, NR), 0) == rcol_off + B)
    link_turn = ones(iota((NR, 128), 1) == rrow_off + B)
    diag = exact(qq[...], diag_tile)
    above = exact(qq[:, 0:128], link_tile)
    below = exact(qq[:, 0:128], link_turn, ((1,), (1,)), True)
    rotor_plan, stator_plan = plan(scalar_bounds(False), REDUCED_STEPS), plan(scalar_bounds(True), REDUCED_STEPS)
    mid, half_inv, first, scale = (
        jnp.where(stator, jnp.asarray(b, F32), jnp.asarray(a, F32))
        for a, b in zip(
            (rotor_plan[0], 1.0 / rotor_plan[1], rotor_plan[2], rotor_plan[3]),
            (stator_plan[0], 1.0 / stator_plan[1], stator_plan[2], stator_plan[3]),
        )
    )
    same = iota((NR, NR), 0) == iota((NR, NR), 1)
    live = jnp.logical_and(rrow_block < CHAIN, rcol_block < CHAIN)
    red = jnp.where(rcol_block == rrow_block, diag, 0.0)
    red -= jnp.where(rcol_block == rrow_block + 1, above, 0.0)
    red -= jnp.where(rcol_block + 1 == rrow_block, below, 0.0)
    first_scale = jnp.where(stator, jnp.asarray(FIRST_SCALE, F32), jnp.asarray(1.0, F32))
    row_scale, col_scale = (jnp.where(i < B, first_scale, 1.0) for i in (rrow, rcol))
    red = jnp.where(live, red * (row_scale * col_scale), jnp.where(same, mid, 0.0))
    rmat[...] = red
    tred[...] = jnp.where(same, mid - red, -red) * half_inv
    chebyshev(NR, first, half_inv, lhs, rhs, yred, tred, REDUCED_STEPS, False)
    xr = yred[...] * scale
    want = jnp.logical_and(
        jnp.logical_and(iota((128, NR), 1) == iota((128, NR), 0) + B * l, iota((128, NR), 0) < 2 * B),
        iota((128, NR), 1) < B * CHAIN,
    )
    wanted = jnp.where(want, col_scale, 0.0)
    yred[...] = xr
    few = wanted[0:80]
    y = dot3(split(few), split(yred[...]))
    y += dot((few - dot3(split(y), split(rmat[...]))).astype(BF16), yred[...].astype(BF16))
    y += dot((few - dot(y, rmat[...], HIGHEST)).astype(BF16), yred[...].astype(BF16))
    yt_h[80:128], yt_l[80:128] = jnp.zeros((48, NR), BF16), jnp.zeros((48, NR), BF16)
    yt_h[0:80], yt_l[0:80] = split(y * col_scale)

    finish(0)

    place_edges(1)
    send_edges(1)
    sides(1)
    edges(1)
    interface(1)
    add_edges()
    finish(1)
    out_ref[pl.ds(0, B, stride=CELLS), :] = f_ref[NI : NI + B, :]
    for m in range(7):
        out_ref[pl.ds(m + 1, B, stride=CELLS), :] = f_ref[B * m : B * m + B, :]

    for t in range(2):
        for copy in list(edge_copies(t)) + end_copies(t, *ends_of) + end_copies(t, *corrections):
            copy.wait_send()
    for copy in kq_copies():
        copy.wait_send()

    @pl.when(outlet)
    def _():
        for t in range(2):
            for copy in f63_copies(t) + late_copies(t):
                copy.wait_send()
        c63_copy(p + 1).wait_send()

    @pl.when(inlet)
    def _():
        for t in range(2):
            pass_copy(t).wait_send()
            f64_copy(t).wait_send()
            for copy in late_copies(t):
                copy.wait_send()


def body(pitches, field, source, couple, shift, gain, row_map, slide):
    zs = pitches // 2
    vmem = pl.BlockSpec(memory_space=pltpu.VMEM)
    dma = pltpu.SemaphoreType.DMA
    V = pltpu.VMEM
    shapes = [(B * CELLS, LINES), (B * CELLS, LINES), (B * CELLS, B), (CELLS, B), (CELLS, B)]
    shapes = [V(s, F32) for s in shapes] + [V((pitches, LINES), I32), V((1, INST), I32)]
    out = pl.pallas_call(
        functools.partial(kernel, pitches),
        out_shape=jax.ShapeDtypeStruct((B * CELLS, LINES), F32),
        in_specs=[pl.BlockSpec(memory_space=pltpu.HBM)] * 7,
        out_specs=vmem,
        scratch_shapes=shapes + [
            V((NF, LINES), F32), V((NF, LINES), F32), V((NF, LINES), F32),
            V((NI, LINES), F32), V((NI, LINES), F32),
            V((NI, B), F32), V((NI, B), F32),
            V((NI, NI), F32), V((NI, NI), F32), V((NI, NI), F32),
            V((4 * NR, NR), BF16), V((2 * NR, NR), BF16),
            V((NF, NI), BF16), V((NF, NI), BF16),
            V((NI, 128), BF16), V((NI, 128), BF16),
            V((128, 128), F32),
            V((NR, NR), F32), V((NR, NR), F32), V((NR, NR), F32),
            V((128, NR), BF16), V((128, NR), BF16),
            V((NR, 256), F32),
            V((NR, LINES), F32), V((B * (CHAIN + 1) + 5, LINES), F32),
            V((2, INST, LINES, LINES), BF16),
            V((INST, zs, 8, LINES), F32),
            V((2, 8, NF), F32), V((2, 2, 8, NF), F32),
            V((CHAIN, 40, 128), F32),
            V((2, CHAIN, 72, LINES), F32), V((2, CHAIN, 8, 128), F32),
            V((2, B, LINES), F32), V((2, B, LINES), F32),
            V((2, zs, B, LINES), F32), V((2, B, LINES), F32),
            V((2, B, LINES), F32), V((2, B, LINES), F32),
            V((B, B), F32), V((B, B), F32), V((2, B, LINES), F32),
            dma((CHAIN,)), dma((CHAIN,)), dma((2, CHAIN)), dma((2, CHAIN)), dma((2, CHAIN)), dma((2, CHAIN)),
            dma((2, 2)), dma((2, 2)), dma((2, zs)), dma((2, zs)),
            dma((2,)), dma((2,)), dma((2,)), dma((2,)), dma, dma,
            dma((2, CHAIN)), dma((2,)), dma((7,)),
        ],
        compiler_params=pltpu.CompilerParams(
            collective_id=0, has_side_effects=True, vmem_limit_bytes=48 * 2**20
        ),
        name="sweeps",
    )(
        *(pltpu.with_memory_space_constraint(x, pltpu.HBM) for x in (
            field.transpose(1, 0, 2).reshape(B * CELLS, LINES),
            source.transpose(1, 0, 2).reshape(B * CELLS, LINES),
            couple.transpose(1, 0, 2).reshape(B * CELLS, B),
            shift, gain, row_map.reshape(pitches, LINES), slide.reshape(1, INST),
        ))
    )
    return out.reshape(B, CELLS, LINES).transpose(1, 0, 2)


def solution(mesh):
    return jax.shard_map(
        functools.partial(body, mesh.shape["pitch"]),
        mesh=mesh,
        in_specs=(
            P("axial", None, "pitch"),
            P("axial", None, "pitch"),
            P("axial", None, None),
            P("axial", None),
            P("axial", None),
            P(),
            P(),
        ),
        out_specs=P("axial", None, "pitch"),
        check_vma=False,
    )
```

```python
import functools
import math

import jax
import jax.numpy as jnp
import numpy as np
from jax import lax
from jax.experimental import pallas as pl
from jax.experimental.pallas import tpu as pltpu
from jax.sharding import PartitionSpec as P

INST, VARS, B = 7, 5, 35
CELLS, LINES, CHAIN = 8, 128, 8
NI = 256
NR = 288
NF = 384
F32, BF16, I32 = jnp.float32, jnp.bfloat16, jnp.int32
HIGHEST = lax.Precision.HIGHEST
MESH = pl.DeviceIdType.MESH

C_LOW, C_HIGH, G_LOW, G_HIGH = 0.299, 5.51, 0.00109, 0.00352
LOCAL_STEPS, REDUCED_STEPS = 7, 6
FIRST_SCALE = 0.5


def scalar_bounds(stator):
    ends = []
    for c, g in ((C_LOW, G_LOW), (C_HIGH, G_HIGH)):
        n = CELLS * CHAIN
        t = np.diag(np.full(n, 2 * c + g)) - c * np.eye(n, k=1) - c * np.eye(n, k=-1)
        if not stator:
            t[0, 0] -= c
        keep = np.arange(0, n, CELLS)
        scale = np.where(np.arange(CHAIN) == 0, FIRST_SCALE if stator else 1.0, 1.0)
        rest = np.setdiff1d(np.arange(n), keep)
        s = t[np.ix_(keep, keep)] - t[np.ix_(keep, rest)] @ np.linalg.solve(
            t[np.ix_(rest, rest)], t[np.ix_(rest, keep)]
        )
        ends.append(np.linalg.eigvalsh(scale[:, None] * s * scale[None, :]))
    return float(ends[0][0]), float(ends[1][-1])


def local_bounds():
    bend = 2 * math.cos(math.pi / CELLS)
    return C_LOW * (2 - bend) + G_LOW, C_HIGH * (2 + bend) + G_HIGH


def plan(bounds, steps):
    low, high = bounds
    mid, half = 0.5 * (high + low), 0.5 * (high - low)
    t = first = mid / half
    for _ in range(steps):
        t = 2 * t * t - 1
    return mid, half, first, 1.0 / t


def dot(a, b, precision=None, dims=((1,), (0,))):
    return lax.dot_general(a, b, (dims, ((), ())), precision=precision, preferred_element_type=F32)


def split(x):
    high = x.astype(BF16)
    return high, (x - high.astype(F32)).astype(BF16)


def dot3(a, b):
    (ah, al), (bh, bl) = a, b
    return dot(ah, bh) + (dot(ah, bl) + dot(al, bh))


def exact(a, pick, dims=((1,), (0,)), swap=False, parts=3):
    pick, total = pick.astype(BF16), None
    for _ in range(parts):
        piece = a.astype(BF16)
        a = a - piece.astype(F32)
        term = dot(pick, piece, None, dims) if swap else dot(piece, pick, None, dims)
        total = term if total is None else total + term
    return total


def iota(shape, axis):
    return lax.broadcasted_iota(I32, shape, axis)


def block_of(index, count):
    return sum(((index >= B * k).astype(I32) for k in range(1, count)), jnp.zeros_like(index))


def ones(mask):
    return jnp.where(mask, 1.0, 0.0).astype(F32)


def chebyshev(n, t, half_inv, lhs, rhs, y_ref, t_ref, steps, exact):
    m = min(n, 256)
    rows = 4 if exact else 3
    eye = ones(iota((n, n), 0) == iota((n, n), 1))

    def load(with_y):
        th, tl = split(t_ref[...])
        lhs[0:n, 0:n] = th
        lhs[n : 2 * n, 0:n] = tl
        rhs[0:n, 0:n] = th
        rhs[n : 2 * n, 0:n] = tl
        if with_y and exact:
            lhs[2 * n : 3 * n, 0:n], lhs[3 * n : 4 * n, 0:n] = split(y_ref[...])
        elif with_y:
            lhs[2 * n : 3 * n, 0:n] = y_ref[...].astype(BF16)

    def corner(block, part):
        if n == m:
            return None
        return dot(lhs[block * n + m : block * n + n, 0:n], rhs[part * n : part * n + n, m:n])

    def times(first, last, part=0):
        return dot(lhs[first * n : last * n, 0:n], rhs[part * n : part * n + n, 0:m])

    def put(ref, update, main, rest):
        value = update(ref[:, 0:m], main, eye[:, 0:m])
        if n > m:
            end = update(ref[m:n, m:n], rest, eye[0 : n - m, 0 : n - m])
            ref[0:m, m:n] = value[m:n].T
            ref[m:n, m:n] = end
        ref[:, 0:m] = value

    def squared(big):
        main = big[0:n] + (big[n : 2 * n] + times(0, 1, 1))
        return main, None if n == m else corner(0, 0) + (corner(1, 0) + corner(0, 1))

    def turn(_, square, one):
        return 2.0 * square - one

    load(False)
    square = squared(times(0, 2))
    y_ref[...] = (2.0 * half_inv) * (t * eye + t_ref[...])
    put(t_ref, turn, *square)
    t = 2.0 * t * t - 1.0

    def grow(t, big):
        mixed, rest = big[0:n], corner(2, 0)
        if exact:
            mixed = mixed + (big[n : 2 * n] + times(2, 3, 1))
        put(y_ref, lambda y, product, _: 2.0 * (t * y + product), mixed, rest)

    def step(_, t):
        load(True)
        big = times(0, rows)
        square = squared(big)
        grow(t, big[2 * n :])
        put(t_ref, turn, *square)
        return 2.0 * t * t - 1.0

    t = lax.fori_loop(0, steps - 2, step, t)
    load(True)
    grow(t, times(2, rows))


def kernel(
    pitches,
    *refs,
):
    args, (out_ref, *args_v) = refs[:7], refs[7:15]
    (
        f_ref, s_ref, r_ref, g_ref, h_ref, cl_ref, cr_ref, smat, ymat, tmat, lhs, rhs, xw_h, xw_l, w_h, w_l, u_ref,
        rmat, yred, tred, yt_h, yt_l, qq, pa, pb, hot, xin,
        edge_send, edge_recv, kq, ab, corr, pass_out, pass_in, f63, f63_out, f64, f64_out, c63, c63_out, late,
        kq_s, kq_r, ab_s, ab_r, co_s, co_r, ed_s, ed_r, f63_s, f63_r, fw_s, fw_r, f64_s, f64_r, c63_s, c63_r, late_s, late_r, in_s,
    ) = refs[15:]
    field_v, source_v, couple_v, shift_v, gain_v, map_v, slide_v = args_v
    p, q = lax.axis_index("axial"), lax.axis_index("pitch")
    l = lax.rem(p, CHAIN)
    base = p - l
    stator = base > 0
    outlet, inlet = p == CHAIN - 1, p == CHAIN
    zs = pitches // 2
    core = lax.rem(q, 2)
    z = q // 2
    left, right = lax.rem(q + pitches - 1, pitches), lax.rem(q + 1, pitches)

    def at(axial, pitch):
        return {"axial": axial, "pitch": pitch}

    def remote(src, dst, send, recv, axial, pitch):
        return pltpu.make_async_remote_copy(
            src_ref=src, dst_ref=dst, send_sem=send, recv_sem=recv,
            device_id=at(axial, pitch), device_id_type=MESH,
        )

    loads = [pltpu.make_async_copy(args[i], args_v[i], in_s.at[i]) for i in range(7)]
    for load in loads:
        load.start()

    barrier = pltpu.get_barrier_semaphore()

    def greet(axial, pitch):
        pl.semaphore_signal(barrier, inc=1, device_id=at(axial, pitch), device_id_type=MESH)

    for d in range(1, CHAIN):
        greet(base + lax.rem(l + d, CHAIN), q)
    greet(p, left)
    greet(p, right)

    @pl.when(outlet)
    def _():
        greet(p + 1, q)

    @pl.when(inlet)
    def _():
        for d in range(zs):
            greet(p - 1, 2 * lax.rem(z + d, zs) + core)

    row = iota((NF, 1), 0)
    row_block = jnp.where(row < 245, block_of(row, 7), 0)
    in_sep = jnp.logical_and(row >= NI, row < NI + B)
    row_off = jnp.where(in_sep, row - NI, row - B * row_block)
    row_cell = jnp.where(row < 245, row_block + 1, jnp.where(in_sep, 0, -1))
    lane = iota((1, LINES), 1)

    def cell_of(src, i):
        return src[pl.ds(i, B, stride=CELLS), :]

    def stack(dst, src):
        dst[240:NF, :] = jnp.zeros((NF - 240, LINES), F32)
        for m in range(7):
            dst[B * m : B * m + B, :] = cell_of(src, m + 1)
        dst[NI : NI + B, :] = cell_of(src, 0)

    loads[0].wait()
    f63_out[0] = cell_of(field_v, CELLS - 1)
    f64_out[0] = cell_of(field_v, 0)
    loads[2].wait()
    c63_out[...] = cell_of(couple_v, CELLS - 1)

    def place_edges(t):
        pick = jnp.logical_or(
            jnp.logical_and(iota((8, LINES), 0) == 0, iota((8, LINES), 1) == 0),
            jnp.logical_and(iota((8, LINES), 0) == 1, iota((8, LINES), 1) == LINES - 1),
        )
        edge_send[t] = exact(f_ref[...], ones(pick), ((1,), (1,)), True, 2)

    for i in (1, 3, 4, 5, 6):
        loads[i].wait()

    def edge_copies(t):
        return (
            remote(edge_send.at[t], edge_recv.at[t, 1], ed_s.at[t, 0], ed_r.at[t, 1], p, left),
            remote(edge_send.at[t], edge_recv.at[t, 0], ed_s.at[t, 1], ed_r.at[t, 0], p, right),
        )

    def f63_copies(t):
        src = f63_out.at[t]
        return [
            remote(src, f63.at[t, z], f63_s.at[t, d], f63_r.at[t, d], p + 1, 2 * lax.rem(z + d, zs) + core)
            for d in range(zs)
        ]

    def f63_arrivals(t):
        src = f63_out.at[t]
        return [
            remote(src, f63.at[t, lax.rem(z + zs - d, zs)], f63_s.at[t, d], f63_r.at[t, d], p - 1, q)
            for d in range(zs)
        ]

    def pass_copy(t):
        return remote(pass_out.at[t], pass_in.at[t], fw_s.at[t], fw_r.at[t], p, q + 1 - 2 * core)

    def f64_copy(t):
        src = f64_out.at[t]
        return remote(src, f64.at[t], f64_s.at[t], f64_r.at[t], p - 1, q)

    def f64_arrival(t):
        src = f64_out.at[t]
        return remote(src, f64.at[t], f64_s.at[t], f64_r.at[t], p + 1, q)

    def c63_copy(to):
        return remote(c63_out, c63, c63_s, c63_r, to, q)

    def kq_copies():
        return [
            remote(kq.at[l], kq.at[l], kq_s.at[d], kq_r.at[d], base + lax.rem(l + d, CHAIN), q)
            for d in range(1, CHAIN)
        ]

    def kq_arrivals():
        peers = [lax.rem(l + CHAIN - d, CHAIN) for d in range(1, CHAIN)]
        return [remote(kq.at[s], kq.at[s], kq_s.at[d + 1], kq_r.at[d + 1], base + s, q) for d, s in enumerate(peers)]

    def end_copies(t, ref, send, recv):
        return [
            remote(ref.at[t, l], ref.at[t, l], send.at[t, d], recv.at[t, d], base + lax.rem(l + d, CHAIN), q)
            for d in range(1, CHAIN)
        ]

    def end_arrivals(t, ref, send, recv):
        peers = [lax.rem(l + CHAIN - d, CHAIN) for d in range(1, CHAIN)]
        return [
            remote(ref.at[t, s], ref.at[t, s], send.at[t, d + 1], recv.at[t, d + 1], base + s, q)
            for d, s in enumerate(peers)
        ]

    ends_of, corrections = (ab, ab_s, ab_r), (corr, co_s, co_r)

    def send_inlet(t):
        @pl.when(inlet)
        def _():
            f64_copy(t).start()

    def send_outlet(t):
        @pl.when(outlet)
        def _():
            for copy in f63_copies(t):
                copy.start()

    def send_edges(t):
        for copy in edge_copies(t):
            copy.start()

    def late_copies(t):
        return [
            remote(late.at[t], late.at[t], late_s.at[t, d], late_r.at[t], base + lax.rem(l + d, CHAIN), q)
            for d in range(1, CHAIN)
        ]

    def late_arrival(t):
        return remote(late.at[t], late.at[t], late_s.at[t, 0], late_r.at[t], jnp.where(stator, CHAIN, CHAIN - 1), q)

    pick_cell = ones(row_cell == iota((NF, CELLS), 1))
    own = row_off == iota((NF, B), 1)
    gain_col = jnp.sum(jnp.where(own, dot(pick_cell, gain_v[...], HIGHEST), 0.0), 1, keepdims=True)
    shift_col = jnp.sum(jnp.where(own, dot(pick_cell, shift_v[...], HIGHEST), 0.0), 1, keepdims=True)
    g_col = shift_col + 2.0 * gain_col

    cl_ref[240:NI, :] = jnp.zeros((NI - 240, B), F32)
    cr_ref[240:NI, :] = jnp.zeros((NI - 240, B), F32)
    for m in range(7):
        cl_ref[B * m : B * m + B, :] = cell_of(couple_v, m)
        cr_ref[B * m : B * m + B, :] = cell_of(couple_v, m + 1)
    col = iota((1, NI), 1)
    col_block = block_of(col, 8)
    tile = ones(iota((B, NI), 0) == col - B * col_block)
    rep_l = exact(cl_ref[...], tile)
    rep_r = exact(cr_ref[...], tile)
    in_block = block_of(iota((NI, 1), 0), 8)
    mid, half, first, scale = plan(local_bounds(), LOCAL_STEPS)
    g_in = g_col[0:NI]
    same = iota((NI, NI), 0) == iota((NI, NI), 1)
    s_full = jnp.where(in_block == col_block, rep_l + rep_r, 0.0)
    s_full -= jnp.where(col_block == in_block + 1, rep_r, 0.0)
    s_full -= jnp.where(col_block + 1 == in_block, rep_l, 0.0)
    s_full += jnp.where(same, jnp.where(iota((NI, 1), 0) < 245, g_in, mid), 0.0)
    s_full = jnp.where(jnp.logical_and(in_block == 7, jnp.logical_not(same)), 0.0, s_full)
    s_full = jnp.where(jnp.logical_and(col_block == 7, jnp.logical_not(same)), 0.0, s_full)
    smat[...] = s_full
    tmat[...] = jnp.where(same, mid - s_full, -s_full) * (1.0 / half)
    links = jnp.where(jnp.logical_and(in_block == 0, col_block == 0), rep_l, 0.0)
    links += jnp.where(jnp.logical_and(in_block == 6, col_block == 1), rep_r, 0.0)
    links = links[:, 0:128]
    links += jnp.where(iota((NI, 128), 1) == row_off[0:NI] + 2 * B, g_in, 0.0)
    chebyshev(NI, jnp.asarray(first, F32), 1.0 / half, lhs, rhs, ymat, tmat, LOCAL_STEPS, True)
    pl.semaphore_wait(barrier, CHAIN + 1 + jnp.where(outlet, zs, 0) + jnp.where(inlet, 1, 0))
    send_outlet(0)
    send_inlet(0)

    @pl.when(outlet)
    def _():
        c63_copy(p + 1).start()

    x0 = ymat[...] * scale
    ymat[...] = x0
    rest = jnp.where(same, 1.0, 0.0) - dot(smat[...], ymat[...], HIGHEST)
    inv = x0 + dot(x0.astype(BF16), rest.astype(BF16))
    xw_h[0:NI], xw_l[0:NI] = split(inv)
    w = dot3((xw_h[0:NI], xw_l[0:NI]), split(links))
    xw_h[NI:NF], xw_l[NI:NF] = split(w.T)
    w_h[...], w_l[...] = split(w)
    u_ref[...] = dot3(split(links.T), (w_h[...], w_l[...]))

    fr, to = iota((128, 128), 0), iota((128, 128), 1)
    top = ones(jnp.logical_or(
        jnp.logical_and(to < B, jnp.logical_or(fr == to + B, fr == to + 2 * B)),
        jnp.logical_and(jnp.logical_and(to >= B, to < 2 * B), fr == to),
    ))
    low = ones(jnp.logical_and(
        jnp.logical_and(to >= 2 * B, to < 3 * B), jnp.logical_or(fr == to - 2 * B, fr == to)
    ))
    sep_g = g_col[NI : NI + 40]
    part = exact(u_ref[0:40, :], top) + exact(u_ref[B : B + 40, :], low)
    part += jnp.where(iota((40, 128), 0) == iota((40, 128), 1), sep_g, 0.0)
    kq[l] = part

    @pl.when(inlet)
    def _():
        c63_copy(p - 1).wait_recv()
        kq[l, 0:B, 0:B] = kq[l, 0:B, 0:B] + c63[...]

    for copy in kq_copies():
        copy.start()

    stack(f_ref, field_v)
    place_edges(0)
    send_edges(0)
    stack(s_ref, source_v)
    place = iota((1, NF), 1)
    place_block = jnp.where(place < 245, block_of(place, 7), 0)
    place_sep = jnp.logical_and(place >= NI, place < NI + B)
    place_off = jnp.where(place_sep, place - NI, place - B * place_block)
    place_cell = jnp.where(place < 245, place_block + 1, jnp.where(place_sep, 0, -1))
    gains = dot(gain_v[...], ones(place_cell == iota((CELLS, NF), 0)), HIGHEST, ((0,), (0,)))
    gain_row = jnp.sum(jnp.where(place_off == iota((B, NF), 0), gains, 0.0), 0, keepdims=True)

    @pl.when(inlet)
    def _():
        lines = map_v[pl.ds(q, 1), :]
        xin[...] = jnp.zeros_like(xin)
        other_lines = map_v[pl.ds(q + 1 - 2 * core, 1), :]
        for whose, wanted_lines in enumerate((lines, other_lines)):
            for a in range(INST):
                found = lax.rem(wanted_lines + slide_v[:, a : a + 1], pitches * LINES)
                hot[whose, a] = ones(iota((LINES, LINES), 0) == lax.rem(found, LINES)).astype(BF16)


    def send_ends(t):
        for copy in end_copies(t, *ends_of):
            copy.start()

    def send_corrections(t):
        for copy in end_copies(t, *corrections):
            copy.start()

    def sides(t):
        f = f_ref[...]
        near = jnp.where(lane == 0, 0.0, pltpu.roll(f, 1, 1)) + jnp.where(
            lane == LINES - 1, 0.0, pltpu.roll(f, LINES - 1, 1)
        )
        r_ref[...] = s_ref[...] + gain_col * near
        both = dot3((xw_h[...], xw_l[...]), split(r_ref[0:NI, :]))
        ab[t, l] = (both[NI:NF] + r_ref[NI:NF, :])[0:72]
        if t == 1:
            send_ends(t)
        r_ref[0:NI, :] = both[0:NI]

    def edges(t):
        for copy in reversed(edge_copies(t)):
            copy.wait_recv()
        ge = edge_recv[t].reshape(16, NF) * gain_row
        ge_h, ge_l = split(ge)
        short = dot3((ge_h[:, 0:NI], ge_l[:, 0:NI]), (w_h[...], w_l[...])) + ge[:, NI:NF]
        which = iota((8, 128), 0)
        corr[t, l] = jnp.where(which == 1, short[0:8], 0.0) + jnp.where(which == 0, short[8:16], 0.0)
        if t == 1:
            send_corrections(t)
        spot = jnp.logical_or(
            jnp.logical_and(iota((16, LINES), 0) == 1, iota((16, LINES), 1) == 0),
            jnp.logical_and(iota((16, LINES), 0) == 8, iota((16, LINES), 1) == LINES - 1),
        )
        added = exact(ge[:, 0:NI].T, ones(spot), parts=2)
        g_ref[...] = added

    def add_edges():
        r_ref[0:NI, :] = r_ref[0:NI, :] + dot3((xw_h[0:NI], xw_l[0:NI]), split(g_ref[...]))

    def send_late(t):
        for copy in late_copies(t):
            copy.start()

    def meet_stator(t):
        f64_arrival(t).wait_recv()
        h_ref[0:208, :] = jnp.zeros((208, LINES), F32)
        h_ref[240:NI, :] = jnp.zeros((NI - 240, LINES), F32)
        h_ref[208:216, :] = jnp.zeros((8, LINES), F32)
        h_ref[210:245, :] = dot(c63_out[...], f64[t], HIGHEST)
        both = dot3((xw_h[...], xw_l[...]), split(h_ref[...]))
        late[t] = both[NI : NI + B]
        send_late(t)
        r_ref[0:NI, :] = r_ref[0:NI, :] + both[0:NI]

    def collect(t, whose, dst):
        lines = map_v[pl.ds(q if whose == 0 else q + 1 - 2 * core, 1), :]
        for a in range(INST):
            high, low_part = split(xin[a].reshape(zs * 8, LINES))
            found = lax.rem(lines + slide_v[:, a : a + 1], pitches * LINES) // LINES
            got = (dot(high, hot[whose, a]) + dot(low_part, hot[whose, a])).reshape(zs, 8, LINES)
            which = 2 * iota((zs, 1, LINES), 0) + core == found.reshape(1, 1, LINES)
            dst[VARS * a : VARS * a + VARS, :] = jnp.sum(jnp.where(which, got, 0.0), 0)[0:VARS]

    def meet_rotor(t):
        for copy in f63_arrivals(t):
            copy.wait_recv()
        for a in range(INST):
            xin[a, :, 0:VARS, :] = f63[t, :, VARS * a : VARS * a + VARS, :]
        collect(t, 1, pass_out.at[t])
        pass_copy(t).start()
        collect(t, 0, u_ref)

    def meet_both(t):
        pass_copy(t).wait_recv()
        late[t] = dot(c63[...], u_ref[0:B, :] + pass_in[t], HIGHEST)
        send_late(t)

    def interface(t):
        @pl.when(outlet)
        def _():
            meet_stator(t)

        @pl.when(inlet)
        def _():
            if t == 1:
                meet_rotor(t)
            meet_both(t)

    def finish(t):
        for copy in end_arrivals(t, *ends_of) + end_arrivals(t, *corrections):
            copy.wait_recv()
        spread = exact(corr[t].reshape(8 * CHAIN, 128).T, spread_pick, parts=2)
        for s in range(CHAIN):
            piece = spread[:, LINES * s : LINES * s + LINES]
            pa[B * s : B * s + B, :] = ab[t, s, 0:B, :] + piece[0:B]
            pb[B * s + B : B * s + 2 * B, :] = ab[t, s, B : 2 * B, :] + piece[B : 2 * B]

        @pl.when(jnp.logical_not(jnp.logical_or(inlet, outlet)))
        def _():
            late_arrival(t).wait_recv()

        @pl.when(stator)
        def _():
            pa[0:B, :] = pa[0:B, :] + late[t]

        @pl.when(jnp.logical_not(stator))
        def _():
            pa[B * (CHAIN - 1) : B * CHAIN, :] = pa[B * (CHAIN - 1) : B * CHAIN, :] + late[t]

        ends = dot3((yt_h[...], yt_l[...]), split(pa[...] + pb[0:NR, :]))
        if t == 0:
            f64_out[1] = ends[0:B]
            send_inlet(1)

            @pl.when(outlet)
            def _():
                h_ref[208:NI, :] = r_ref[208:NI, :] + dot3((w_h[208:NI], w_l[208:NI]), split(ends))
                f63_out[1] = h_ref[210:245, :]

            send_outlet(1)
        f_ref[0:NI, :] = r_ref[0:NI, :] + dot3((w_h[...], w_l[...]), split(ends))
        f_ref[NI:NF, :] = ends

    sides(0)
    edges(0)
    add_edges()

    @pl.when(inlet)
    def _():
        meet_rotor(0)

    pb[0:B, :] = jnp.zeros((B, LINES), F32)
    pa[B * CHAIN : NR, :] = jnp.zeros((NR - B * CHAIN, LINES), F32)
    lines_at, pick_at = iota((8 * CHAIN, LINES * CHAIN), 1), iota((8 * CHAIN, LINES * CHAIN), 0)
    spread_pick = ones(jnp.logical_or(
        lines_at == LINES * (pick_at // 8) + jnp.where(lax.rem(pick_at, 8) == 1, 0, -1 - LINES * CHAIN),
        lines_at == LINES * (pick_at // 8) + jnp.where(lax.rem(pick_at, 8) == 0, LINES - 1, -1 - LINES * CHAIN),
    )).astype(BF16)

    for copy in kq_arrivals():
        copy.wait_recv()
    send_ends(0)
    send_corrections(0)
    interface(0)
    qq[0:B, 128:256] = jnp.zeros((B, 128), F32)
    qq[B * CHAIN : NR, :] = jnp.zeros((NR - B * CHAIN, 256), F32)
    for s in range(CHAIN):
        qq[B * s : B * s + B, 0:128] = kq[s, 0:B, :]
        if s + 1 < CHAIN:
            qq[B * s + B : B * s + 2 * B, 128:256] = kq[s, 0:B, :]
    rcol, rrow = iota((1, NR), 1), iota((NR, 1), 0)
    rcol_block, rrow_block = block_of(rcol, 9), block_of(rrow, 9)
    rcol_off, rrow_off = rcol - B * rcol_block, rrow - B * rrow_block
    source_row = iota((256, NR), 0)
    diag_tile = ones(jnp.logical_or(source_row == rcol_off, source_row == rcol_off + 128 + 2 * B))
    link_tile = ones(iota((128, NR), 0) == rcol_off + B)
    link_turn = ones(iota((NR, 128), 1) == rrow_off + B)
    diag = exact(qq[...], diag_tile)
    above = exact(qq[:, 0:128], link_tile)
    below = exact(qq[:, 0:128], link_turn, ((1,), (1,)), True)
    rotor_plan, stator_plan = plan(scalar_bounds(False), REDUCED_STEPS), plan(scalar_bounds(True), REDUCED_STEPS)
    mid, half_inv, first, scale = (
        jnp.where(stator, jnp.asarray(b, F32), jnp.asarray(a, F32))
        for a, b in zip(
            (rotor_plan[0], 1.0 / rotor_plan[1], rotor_plan[2], rotor_plan[3]),
            (stator_plan[0], 1.0 / stator_plan[1], stator_plan[2], stator_plan[3]),
        )
    )
    same = iota((NR, NR), 0) == iota((NR, NR), 1)
    live = jnp.logical_and(rrow_block < CHAIN, rcol_block < CHAIN)
    red = jnp.where(rcol_block == rrow_block, diag, 0.0)
    red -= jnp.where(rcol_block == rrow_block + 1, above, 0.0)
    red -= jnp.where(rcol_block + 1 == rrow_block, below, 0.0)
    first_scale = jnp.where(stator, jnp.asarray(FIRST_SCALE, F32), jnp.asarray(1.0, F32))
    row_scale, col_scale = (jnp.where(i < B, first_scale, 1.0) for i in (rrow, rcol))
    red = jnp.where(live, red * (row_scale * col_scale), jnp.where(same, mid, 0.0))
    rmat[...] = red
    tred[...] = jnp.where(same, mid - red, -red) * half_inv
    chebyshev(NR, first, half_inv, lhs, rhs, yred, tred, REDUCED_STEPS, False)
    xr = yred[...] * scale
    want = jnp.logical_and(
        jnp.logical_and(iota((128, NR), 1) == iota((128, NR), 0) + B * l, iota((128, NR), 0) < 2 * B),
        iota((128, NR), 1) < B * CHAIN,
    )
    wanted = jnp.where(want, col_scale, 0.0)
    yred[...] = xr
    few = wanted[0:80]
    y = dot3(split(few), split(yred[...]))
    y += dot((few - dot3(split(y), split(rmat[...]))).astype(BF16), yred[...].astype(BF16))
    y += dot((few - dot(y, rmat[...], HIGHEST)).astype(BF16), yred[...].astype(BF16))
    yt_h[80:128], yt_l[80:128] = jnp.zeros((48, NR), BF16), jnp.zeros((48, NR), BF16)
    yt_h[0:80], yt_l[0:80] = split(y * col_scale)

    finish(0)

    place_edges(1)
    send_edges(1)
    sides(1)
    edges(1)
    interface(1)
    add_edges()
    finish(1)
    out_ref[pl.ds(0, B, stride=CELLS), :] = f_ref[NI : NI + B, :]
    for m in range(7):
        out_ref[pl.ds(m + 1, B, stride=CELLS), :] = f_ref[B * m : B * m + B, :]

    for t in range(2):
        for copy in list(edge_copies(t)) + end_copies(t, *ends_of) + end_copies(t, *corrections):
            copy.wait_send()
    for copy in kq_copies():
        copy.wait_send()

    @pl.when(outlet)
    def _():
        for t in range(2):
            for copy in f63_copies(t) + late_copies(t):
                copy.wait_send()
        c63_copy(p + 1).wait_send()

    @pl.when(inlet)
    def _():
        for t in range(2):
            pass_copy(t).wait_send()
            f64_copy(t).wait_send()
            for copy in late_copies(t):
                copy.wait_send()


def body(pitches, field, source, couple, shift, gain, row_map, slide):
    zs = pitches // 2
    vmem = pl.BlockSpec(memory_space=pltpu.VMEM)
    dma = pltpu.SemaphoreType.DMA
    V = pltpu.VMEM
    shapes = [(B * CELLS, LINES), (B * CELLS, LINES), (B * CELLS, B), (CELLS, B), (CELLS, B)]
    shapes = [V(s, F32) for s in shapes] + [V((pitches, LINES), I32), V((1, INST), I32)]
    out = pl.pallas_call(
        functools.partial(kernel, pitches),
        out_shape=jax.ShapeDtypeStruct((B * CELLS, LINES), F32),
        in_specs=[pl.BlockSpec(memory_space=pltpu.HBM)] * 7,
        out_specs=vmem,
        scratch_shapes=shapes + [
            V((NF, LINES), F32), V((NF, LINES), F32), V((NF, LINES), F32),
            V((NI, LINES), F32), V((NI, LINES), F32),
            V((NI, B), F32), V((NI, B), F32),
            V((NI, NI), F32), V((NI, NI), F32), V((NI, NI), F32),
            V((4 * NR, NR), BF16), V((2 * NR, NR), BF16),
            V((NF, NI), BF16), V((NF, NI), BF16),
            V((NI, 128), BF16), V((NI, 128), BF16),
            V((128, 128), F32),
            V((NR, NR), F32), V((NR, NR), F32), V((NR, NR), F32),
            V((128, NR), BF16), V((128, NR), BF16),
            V((NR, 256), F32),
            V((NR, LINES), F32), V((B * (CHAIN + 1) + 5, LINES), F32),
            V((2, INST, LINES, LINES), BF16),
            V((INST, zs, 8, LINES), F32),
            V((2, 8, NF), F32), V((2, 2, 8, NF), F32),
            V((CHAIN, 40, 128), F32),
            V((2, CHAIN, 72, LINES), F32), V((2, CHAIN, 8, 128), F32),
            V((2, B, LINES), F32), V((2, B, LINES), F32),
            V((2, zs, B, LINES), F32), V((2, B, LINES), F32),
            V((2, B, LINES), F32), V((2, B, LINES), F32),
            V((B, B), F32), V((B, B), F32), V((2, B, LINES), F32),
            dma((CHAIN,)), dma((CHAIN,)), dma((2, CHAIN)), dma((2, CHAIN)), dma((2, CHAIN)), dma((2, CHAIN)),
            dma((2, 2)), dma((2, 2)), dma((2, zs)), dma((2, zs)),
            dma((2,)), dma((2,)), dma((2,)), dma((2,)), dma, dma,
            dma((2, CHAIN)), dma((2,)), dma((7,)),
        ],
        compiler_params=pltpu.CompilerParams(
            collective_id=0, has_side_effects=True, vmem_limit_bytes=48 * 2**20
        ),
        name="sweeps",
    )(
        *(pltpu.with_memory_space_constraint(x, pltpu.HBM) for x in (
            field.transpose(1, 0, 2).reshape(B * CELLS, LINES),
            source.transpose(1, 0, 2).reshape(B * CELLS, LINES),
            couple.transpose(1, 0, 2).reshape(B * CELLS, B),
            shift, gain, row_map.reshape(pitches, LINES), slide.reshape(1, INST),
        ))
    )
    return out.reshape(B, CELLS, LINES).transpose(1, 0, 2)


def solution(mesh):
    return jax.shard_map(
        functools.partial(body, mesh.shape["pitch"]),
        mesh=mesh,
        in_specs=(
            P("axial", None, "pitch"),
            P("axial", None, "pitch"),
            P("axial", None, None),
            P("axial", None),
            P("axial", None),
            P(),
            P(),
        ),
        out_specs=P("axial", None, "pitch"),
        check_vma=False,
    )
```

```python
import functools
import math

import jax
import jax.numpy as jnp
import numpy as np
from jax import lax
from jax.experimental import pallas as pl
from jax.experimental.pallas import tpu as pltpu
from jax.sharding import PartitionSpec as P

INST, VARS, B = 7, 5, 35
CELLS, LINES, CHAIN = 8, 128, 8
NI = 256
NR = 288
NF = 384
F32, BF16, I32 = jnp.float32, jnp.bfloat16, jnp.int32
HIGHEST = lax.Precision.HIGHEST
MESH = pl.DeviceIdType.MESH

C_LOW, C_HIGH, G_LOW, G_HIGH = 0.299, 5.51, 0.00109, 0.00352
LOCAL_STEPS, REDUCED_STEPS = 7, 6
FIRST_SCALE = 0.5


def scalar_bounds(stator):
    ends = []
    for c, g in ((C_LOW, G_LOW), (C_HIGH, G_HIGH)):
        n = CELLS * CHAIN
        t = np.diag(np.full(n, 2 * c + g)) - c * np.eye(n, k=1) - c * np.eye(n, k=-1)
        if not stator:
            t[0, 0] -= c
        keep = np.arange(0, n, CELLS)
        scale = np.where(np.arange(CHAIN) == 0, FIRST_SCALE if stator else 1.0, 1.0)
        rest = np.setdiff1d(np.arange(n), keep)
        s = t[np.ix_(keep, keep)] - t[np.ix_(keep, rest)] @ np.linalg.solve(
            t[np.ix_(rest, rest)], t[np.ix_(rest, keep)]
        )
        ends.append(np.linalg.eigvalsh(scale[:, None] * s * scale[None, :]))
    return float(ends[0][0]), float(ends[1][-1])


def local_bounds():
    bend = 2 * math.cos(math.pi / CELLS)
    return C_LOW * (2 - bend) + G_LOW, C_HIGH * (2 + bend) + G_HIGH


def plan(bounds, steps):
    low, high = bounds
    mid, half = 0.5 * (high + low), 0.5 * (high - low)
    t = first = mid / half
    for _ in range(steps):
        t = 2 * t * t - 1
    return mid, half, first, 1.0 / t


def dot(a, b, precision=None, dims=((1,), (0,))):
    return lax.dot_general(a, b, (dims, ((), ())), precision=precision, preferred_element_type=F32)


def split(x):
    high = x.astype(BF16)
    return high, (x - high.astype(F32)).astype(BF16)


def dot3(a, b):
    (ah, al), (bh, bl) = a, b
    return dot(ah, bh) + (dot(ah, bl) + dot(al, bh))


def exact(a, pick, dims=((1,), (0,)), swap=False, parts=3):
    pick, total = pick.astype(BF16), None
    for _ in range(parts):
        piece = a.astype(BF16)
        a = a - piece.astype(F32)
        term = dot(pick, piece, None, dims) if swap else dot(piece, pick, None, dims)
        total = term if total is None else total + term
    return total


def iota(shape, axis):
    return lax.broadcasted_iota(I32, shape, axis)


def block_of(index, count):
    return sum(((index >= B * k).astype(I32) for k in range(1, count)), jnp.zeros_like(index))


def ones(mask):
    return jnp.where(mask, 1.0, 0.0).astype(F32)


def chebyshev(n, t, half_inv, lhs, rhs, y_ref, t_ref, steps, exact):
    m = min(n, 256)
    rows = 4 if exact else 3
    eye = ones(iota((n, n), 0) == iota((n, n), 1))

    def load(with_y):
        th, tl = split(t_ref[...])
        lhs[0:n, 0:n] = th
        lhs[n : 2 * n, 0:n] = tl
        rhs[0:n, 0:n] = th
        rhs[n : 2 * n, 0:n] = tl
        if with_y and exact:
            lhs[2 * n : 3 * n, 0:n], lhs[3 * n : 4 * n, 0:n] = split(y_ref[...])
        elif with_y:
            lhs[2 * n : 3 * n, 0:n] = y_ref[...].astype(BF16)

    def corner(block, part):
        if n == m:
            return None
        return dot(lhs[block * n + m : block * n + n, 0:n], rhs[part * n : part * n + n, m:n])

    def times(first, last, part=0):
        return dot(lhs[first * n : last * n, 0:n], rhs[part * n : part * n + n, 0:m])

    def put(ref, update, main, rest):
        value = update(ref[:, 0:m], main, eye[:, 0:m])
        if n > m:
            end = update(ref[m:n, m:n], rest, eye[0 : n - m, 0 : n - m])
            ref[0:m, m:n] = value[m:n].T
            ref[m:n, m:n] = end
        ref[:, 0:m] = value

    def squared(big):
        main = big[0:n] + (big[n : 2 * n] + times(0, 1, 1))
        return main, None if n == m else corner(0, 0) + (corner(1, 0) + corner(0, 1))

    def turn(_, square, one):
        return 2.0 * square - one

    load(False)
    square = squared(times(0, 2))
    y_ref[...] = (2.0 * half_inv) * (t * eye + t_ref[...])
    put(t_ref, turn, *square)
    t = 2.0 * t * t - 1.0

    def grow(t, big):
        mixed, rest = big[0:n], corner(2, 0)
        if exact:
            mixed = mixed + (big[n : 2 * n] + times(2, 3, 1))
        put(y_ref, lambda y, product, _: 2.0 * (t * y + product), mixed, rest)

    def step(_, t):
        load(True)
        big = times(0, rows)
        square = squared(big)
        grow(t, big[2 * n :])
        put(t_ref, turn, *square)
        return 2.0 * t * t - 1.0

    t = lax.fori_loop(0, steps - 2, step, t)
    load(True)
    grow(t, times(2, rows))


def kernel(
    pitches,
    *refs,
):
    args, (out_ref, *args_v) = refs[:7], refs[7:15]
    (
        f_ref, s_ref, r_ref, g_ref, h_ref, cl_ref, cr_ref, smat, ymat, tmat, lhs, rhs, xw_h, xw_l, w_h, w_l, u_ref,
        rmat, yred, tred, yt_h, yt_l, qq, pa, pb, hot, xin,
        edge_send, edge_recv, kq, ab, corr, pass_out, pass_in, f63, f63_out, f64, f64_out, c63, c63_out, late,
        kq_s, kq_r, ab_s, ab_r, co_s, co_r, ed_s, ed_r, f63_s, f63_r, fw_s, fw_r, f64_s, f64_r, c63_s, c63_r, late_s, late_r, in_s,
    ) = refs[15:]
    field_v, source_v, couple_v, shift_v, gain_v, map_v, slide_v = args_v
    p, q = lax.axis_index("axial"), lax.axis_index("pitch")
    l = lax.rem(p, CHAIN)
    base = p - l
    stator = base > 0
    outlet, inlet = p == CHAIN - 1, p == CHAIN
    zs = pitches // 2
    core = lax.rem(q, 2)
    z = q // 2
    left, right = lax.rem(q + pitches - 1, pitches), lax.rem(q + 1, pitches)

    def at(axial, pitch):
        return {"axial": axial, "pitch": pitch}

    def remote(src, dst, send, recv, axial, pitch):
        return pltpu.make_async_remote_copy(
            src_ref=src, dst_ref=dst, send_sem=send, recv_sem=recv,
            device_id=at(axial, pitch), device_id_type=MESH,
        )

    loads = [pltpu.make_async_copy(args[i], args_v[i], in_s.at[i]) for i in range(7)]
    for load in loads:
        load.start()

    barrier = pltpu.get_barrier_semaphore()

    def greet(axial, pitch):
        pl.semaphore_signal(barrier, inc=1, device_id=at(axial, pitch), device_id_type=MESH)

    for d in range(1, CHAIN):
        greet(base + lax.rem(l + d, CHAIN), q)
    greet(p, left)
    greet(p, right)

    @pl.when(outlet)
    def _():
        greet(p + 1, q)

    @pl.when(inlet)
    def _():
        for d in range(zs):
            greet(p - 1, 2 * lax.rem(z + d, zs) + core)

    row = iota((NF, 1), 0)
    row_block = jnp.where(row < 245, block_of(row, 7), 0)
    in_sep = jnp.logical_and(row >= NI, row < NI + B)
    row_off = jnp.where(in_sep, row - NI, row - B * row_block)
    row_cell = jnp.where(row < 245, row_block + 1, jnp.where(in_sep, 0, -1))
    lane = iota((1, LINES), 1)

    def cell_of(src, i):
        return src[pl.ds(i, B, stride=CELLS), :]

    def stack(dst, src):
        dst[240:NF, :] = jnp.zeros((NF - 240, LINES), F32)
        for m in range(7):
            dst[B * m : B * m + B, :] = cell_of(src, m + 1)
        dst[NI : NI + B, :] = cell_of(src, 0)

    loads[0].wait()
    f63_out[0] = cell_of(field_v, CELLS - 1)
    f64_out[0] = cell_of(field_v, 0)
    loads[2].wait()
    c63_out[...] = cell_of(couple_v, CELLS - 1)

    def place_edges(t):
        pick = jnp.logical_or(
            jnp.logical_and(iota((8, LINES), 0) == 0, iota((8, LINES), 1) == 0),
            jnp.logical_and(iota((8, LINES), 0) == 1, iota((8, LINES), 1) == LINES - 1),
        )
        edge_send[t] = exact(f_ref[...], ones(pick), ((1,), (1,)), True, 2)

    for i in (1, 3, 4, 5, 6):
        loads[i].wait()

    def edge_copies(t):
        return (
            remote(edge_send.at[t], edge_recv.at[t, 1], ed_s.at[t, 0], ed_r.at[t, 1], p, left),
            remote(edge_send.at[t], edge_recv.at[t, 0], ed_s.at[t, 1], ed_r.at[t, 0], p, right),
        )

    def f63_copies(t):
        src = f63_out.at[t]
        return [
            remote(src, f63.at[t, z], f63_s.at[t, d], f63_r.at[t, d], p + 1, 2 * lax.rem(z + d, zs) + core)
            for d in range(zs)
        ]

    def f63_arrivals(t):
        src = f63_out.at[t]
        return [
            remote(src, f63.at[t, lax.rem(z + zs - d, zs)], f63_s.at[t, d], f63_r.at[t, d], p - 1, q)
            for d in range(zs)
        ]

    def pass_copy(t):
        return remote(pass_out.at[t], pass_in.at[t], fw_s.at[t], fw_r.at[t], p, q + 1 - 2 * core)

    def f64_copy(t):
        src = f64_out.at[t]
        return remote(src, f64.at[t], f64_s.at[t], f64_r.at[t], p - 1, q)

    def f64_arrival(t):
        src = f64_out.at[t]
        return remote(src, f64.at[t], f64_s.at[t], f64_r.at[t], p + 1, q)

    def c63_copy(to):
        return remote(c63_out, c63, c63_s, c63_r, to, q)

    def kq_copies():
        return [
            remote(kq.at[l], kq.at[l], kq_s.at[d], kq_r.at[d], base + lax.rem(l + d, CHAIN), q)
            for d in range(1, CHAIN)
        ]

    def kq_arrivals():
        peers = [lax.rem(l + CHAIN - d, CHAIN) for d in range(1, CHAIN)]
        return [remote(kq.at[s], kq.at[s], kq_s.at[d + 1], kq_r.at[d + 1], base + s, q) for d, s in enumerate(peers)]

    def end_copies(t, ref, send, recv):
        return [
            remote(ref.at[t, l], ref.at[t, l], send.at[t, d], recv.at[t, d], base + lax.rem(l + d, CHAIN), q)
            for d in range(1, CHAIN)
        ]

    def end_arrivals(t, ref, send, recv):
        peers = [lax.rem(l + CHAIN - d, CHAIN) for d in range(1, CHAIN)]
        return [
            remote(ref.at[t, s], ref.at[t, s], send.at[t, d + 1], recv.at[t, d + 1], base + s, q)
            for d, s in enumerate(peers)
        ]

    ends_of, corrections = (ab, ab_s, ab_r), (corr, co_s, co_r)

    def send_inlet(t):
        @pl.when(inlet)
        def _():
            f64_copy(t).start()

    def send_outlet(t):
        @pl.when(outlet)
        def _():
            for copy in f63_copies(t):
                copy.start()

    def send_edges(t):
        for copy in edge_copies(t):
            copy.start()

    def late_copies(t):
        return [
            remote(late.at[t], late.at[t], late_s.at[t, d], late_r.at[t], base + lax.rem(l + d, CHAIN), q)
            for d in range(1, CHAIN)
        ]

    def late_arrival(t):
        return remote(late.at[t], late.at[t], late_s.at[t, 0], late_r.at[t], jnp.where(stator, CHAIN, CHAIN - 1), q)

    pick_cell = ones(row_cell == iota((NF, CELLS), 1))
    own = row_off == iota((NF, B), 1)
    gain_col = jnp.sum(jnp.where(own, dot(pick_cell, gain_v[...], HIGHEST), 0.0), 1, keepdims=True)
    shift_col = jnp.sum(jnp.where(own, dot(pick_cell, shift_v[...], HIGHEST), 0.0), 1, keepdims=True)
    g_col = shift_col + 2.0 * gain_col

    cl_ref[240:NI, :] = jnp.zeros((NI - 240, B), F32)
    cr_ref[240:NI, :] = jnp.zeros((NI - 240, B), F32)
    for m in range(7):
        cl_ref[B * m : B * m + B, :] = cell_of(couple_v, m)
        cr_ref[B * m : B * m + B, :] = cell_of(couple_v, m + 1)
    col = iota((1, NI), 1)
    col_block = block_of(col, 8)
    tile = ones(iota((B, NI), 0) == col - B * col_block)
    rep_l = exact(cl_ref[...], tile)
    rep_r = exact(cr_ref[...], tile)
    in_block = block_of(iota((NI, 1), 0), 8)
    mid, half, first, scale = plan(local_bounds(), LOCAL_STEPS)
    g_in = g_col[0:NI]
    same = iota((NI, NI), 0) == iota((NI, NI), 1)
    s_full = jnp.where(in_block == col_block, rep_l + rep_r, 0.0)
    s_full -= jnp.where(col_block == in_block + 1, rep_r, 0.0)
    s_full -= jnp.where(col_block + 1 == in_block, rep_l, 0.0)
    s_full += jnp.where(same, jnp.where(iota((NI, 1), 0) < 245, g_in, mid), 0.0)
    s_full = jnp.where(jnp.logical_and(in_block == 7, jnp.logical_not(same)), 0.0, s_full)
    s_full = jnp.where(jnp.logical_and(col_block == 7, jnp.logical_not(same)), 0.0, s_full)
    smat[...] = s_full
    tmat[...] = jnp.where(same, mid - s_full, -s_full) * (1.0 / half)
    links = jnp.where(jnp.logical_and(in_block == 0, col_block == 0), rep_l, 0.0)
    links += jnp.where(jnp.logical_and(in_block == 6, col_block == 1), rep_r, 0.0)
    links = links[:, 0:128]
    links += jnp.where(iota((NI, 128), 1) == row_off[0:NI] + 2 * B, g_in, 0.0)
    pl.semaphore_wait(barrier, CHAIN + 1 + jnp.where(outlet, zs, 0) + jnp.where(inlet, 1, 0))
    send_outlet(0)
    send_inlet(0)

    @pl.when(outlet)
    def _():
        c63_copy(p + 1).start()

    chebyshev(NI, jnp.asarray(first, F32), 1.0 / half, lhs, rhs, ymat, tmat, LOCAL_STEPS, True)
    x0 = ymat[...] * scale
    ymat[...] = x0
    rest = jnp.where(same, 1.0, 0.0) - dot(smat[...], ymat[...], HIGHEST)
    inv = x0 + dot(x0.astype(BF16), rest.astype(BF16))
    xw_h[0:NI], xw_l[0:NI] = split(inv)
    w = dot3((xw_h[0:NI], xw_l[0:NI]), split(links))
    xw_h[NI:NF], xw_l[NI:NF] = split(w.T)
    w_h[...], w_l[...] = split(w)
    u_ref[...] = dot3(split(links.T), (w_h[...], w_l[...]))

    fr, to = iota((128, 128), 0), iota((128, 128), 1)
    top = ones(jnp.logical_or(
        jnp.logical_and(to < B, jnp.logical_or(fr == to + B, fr == to + 2 * B)),
        jnp.logical_and(jnp.logical_and(to >= B, to < 2 * B), fr == to),
    ))
    low = ones(jnp.logical_and(
        jnp.logical_and(to >= 2 * B, to < 3 * B), jnp.logical_or(fr == to - 2 * B, fr == to)
    ))
    sep_g = g_col[NI : NI + 40]
    part = exact(u_ref[0:40, :], top) + exact(u_ref[B : B + 40, :], low)
    part += jnp.where(iota((40, 128), 0) == iota((40, 128), 1), sep_g, 0.0)
    kq[l] = part

    @pl.when(inlet)
    def _():
        c63_copy(p - 1).wait_recv()
        kq[l, 0:B, 0:B] = kq[l, 0:B, 0:B] + c63[...]

    for copy in kq_copies():
        copy.start()

    stack(f_ref, field_v)
    place_edges(0)
    send_edges(0)
    stack(s_ref, source_v)
    place = iota((1, NF), 1)
    place_block = jnp.where(place < 245, block_of(place, 7), 0)
    place_sep = jnp.logical_and(place >= NI, place < NI + B)
    place_off = jnp.where(place_sep, place - NI, place - B * place_block)
    place_cell = jnp.where(place < 245, place_block + 1, jnp.where(place_sep, 0, -1))
    gains = dot(gain_v[...], ones(place_cell == iota((CELLS, NF), 0)), HIGHEST, ((0,), (0,)))
    gain_row = jnp.sum(jnp.where(place_off == iota((B, NF), 0), gains, 0.0), 0, keepdims=True)

    @pl.when(inlet)
    def _():
        lines = map_v[pl.ds(q, 1), :]
        xin[...] = jnp.zeros_like(xin)
        other_lines = map_v[pl.ds(q + 1 - 2 * core, 1), :]
        for whose, wanted_lines in enumerate((lines, other_lines)):
            for a in range(INST):
                found = lax.rem(wanted_lines + slide_v[:, a : a + 1], pitches * LINES)
                hot[whose, a] = ones(iota((LINES, LINES), 0) == lax.rem(found, LINES)).astype(BF16)


    def send_ends(t):
        for copy in end_copies(t, *ends_of):
            copy.start()

    def send_corrections(t):
        for copy in end_copies(t, *corrections):
            copy.start()

    def sides(t):
        f = f_ref[...]
        near = jnp.where(lane == 0, 0.0, pltpu.roll(f, 1, 1)) + jnp.where(
            lane == LINES - 1, 0.0, pltpu.roll(f, LINES - 1, 1)
        )
        r_ref[...] = s_ref[...] + gain_col * near
        both = dot3((xw_h[...], xw_l[...]), split(r_ref[0:NI, :]))
        ab[t, l] = (both[NI:NF] + r_ref[NI:NF, :])[0:72]
        if t == 1:
            send_ends(t)
        r_ref[0:NI, :] = both[0:NI]

    def edges(t):
        for copy in reversed(edge_copies(t)):
            copy.wait_recv()
        ge = edge_recv[t].reshape(16, NF) * gain_row
        ge_h, ge_l = split(ge)
        short = dot3((ge_h[:, 0:NI], ge_l[:, 0:NI]), (w_h[...], w_l[...])) + ge[:, NI:NF]
        which = iota((8, 128), 0)
        corr[t, l] = jnp.where(which == 1, short[0:8], 0.0) + jnp.where(which == 0, short[8:16], 0.0)
        if t == 1:
            send_corrections(t)
        spot = jnp.logical_or(
            jnp.logical_and(iota((16, LINES), 0) == 1, iota((16, LINES), 1) == 0),
            jnp.logical_and(iota((16, LINES), 0) == 8, iota((16, LINES), 1) == LINES - 1),
        )
        added = exact(ge[:, 0:NI].T, ones(spot), parts=2)
        g_ref[...] = added

    def add_edges():
        r_ref[0:NI, :] = r_ref[0:NI, :] + dot3((xw_h[0:NI], xw_l[0:NI]), split(g_ref[...]))

    def send_late(t):
        for copy in late_copies(t):
            copy.start()

    def meet_stator(t):
        f64_arrival(t).wait_recv()
        h_ref[0:208, :] = jnp.zeros((208, LINES), F32)
        h_ref[240:NI, :] = jnp.zeros((NI - 240, LINES), F32)
        h_ref[208:216, :] = jnp.zeros((8, LINES), F32)
        h_ref[210:245, :] = dot(c63_out[...], f64[t], HIGHEST)
        both = dot3((xw_h[...], xw_l[...]), split(h_ref[...]))
        late[t] = both[NI : NI + B]
        send_late(t)
        r_ref[0:NI, :] = r_ref[0:NI, :] + both[0:NI]

    def collect(t, whose, dst):
        lines = map_v[pl.ds(q if whose == 0 else q + 1 - 2 * core, 1), :]
        for a in range(INST):
            high, low_part = split(xin[a].reshape(zs * 8, LINES))
            found = lax.rem(lines + slide_v[:, a : a + 1], pitches * LINES) // LINES
            got = (dot(high, hot[whose, a]) + dot(low_part, hot[whose, a])).reshape(zs, 8, LINES)
            which = 2 * iota((zs, 1, LINES), 0) + core == found.reshape(1, 1, LINES)
            dst[VARS * a : VARS * a + VARS, :] = jnp.sum(jnp.where(which, got, 0.0), 0)[0:VARS]

    def meet_rotor(t):
        for copy in f63_arrivals(t):
            copy.wait_recv()
        for a in range(INST):
            xin[a, :, 0:VARS, :] = f63[t, :, VARS * a : VARS * a + VARS, :]
        collect(t, 1, pass_out.at[t])
        pass_copy(t).start()
        collect(t, 0, u_ref)

    def meet_both(t):
        pass_copy(t).wait_recv()
        late[t] = dot(c63[...], u_ref[0:B, :] + pass_in[t], HIGHEST)
        send_late(t)

    def interface(t):
        @pl.when(outlet)
        def _():
            meet_stator(t)

        @pl.when(inlet)
        def _():
            if t == 1:
                meet_rotor(t)
            meet_both(t)

    def finish(t):
        for copy in end_arrivals(t, *ends_of) + end_arrivals(t, *corrections):
            copy.wait_recv()
        spread = exact(corr[t].reshape(8 * CHAIN, 128).T, spread_pick, parts=2)
        for s in range(CHAIN):
            piece = spread[:, LINES * s : LINES * s + LINES]
            pa[B * s : B * s + B, :] = ab[t, s, 0:B, :] + piece[0:B]
            pb[B * s + B : B * s + 2 * B, :] = ab[t, s, B : 2 * B, :] + piece[B : 2 * B]

        @pl.when(jnp.logical_not(jnp.logical_or(inlet, outlet)))
        def _():
            late_arrival(t).wait_recv()

        @pl.when(stator)
        def _():
            pa[0:B, :] = pa[0:B, :] + late[t]

        @pl.when(jnp.logical_not(stator))
        def _():
            pa[B * (CHAIN - 1) : B * CHAIN, :] = pa[B * (CHAIN - 1) : B * CHAIN, :] + late[t]

        ends = dot3((yt_h[...], yt_l[...]), split(pa[...] + pb[0:NR, :]))
        if t == 0:
            f64_out[1] = ends[0:B]
            send_inlet(1)

            @pl.when(outlet)
            def _():
                h_ref[208:NI, :] = r_ref[208:NI, :] + dot3((w_h[208:NI], w_l[208:NI]), split(ends))
                f63_out[1] = h_ref[210:245, :]

            send_outlet(1)
        f_ref[0:NI, :] = r_ref[0:NI, :] + dot3((w_h[...], w_l[...]), split(ends))
        f_ref[NI:NF, :] = ends

    sides(0)
    edges(0)
    add_edges()

    @pl.when(inlet)
    def _():
        meet_rotor(0)

    pb[0:B, :] = jnp.zeros((B, LINES), F32)
    pa[B * CHAIN : NR, :] = jnp.zeros((NR - B * CHAIN, LINES), F32)
    lines_at, pick_at = iota((8 * CHAIN, LINES * CHAIN), 1), iota((8 * CHAIN, LINES * CHAIN), 0)
    spread_pick = ones(jnp.logical_or(
        lines_at == LINES * (pick_at // 8) + jnp.where(lax.rem(pick_at, 8) == 1, 0, -1 - LINES * CHAIN),
        lines_at == LINES * (pick_at // 8) + jnp.where(lax.rem(pick_at, 8) == 0, LINES - 1, -1 - LINES * CHAIN),
    )).astype(BF16)

    for copy in kq_arrivals():
        copy.wait_recv()
    send_ends(0)
    send_corrections(0)
    interface(0)
    qq[0:B, 128:256] = jnp.zeros((B, 128), F32)
    qq[B * CHAIN : NR, :] = jnp.zeros((NR - B * CHAIN, 256), F32)
    for s in range(CHAIN):
        qq[B * s : B * s + B, 0:128] = kq[s, 0:B, :]
        if s + 1 < CHAIN:
            qq[B * s + B : B * s + 2 * B, 128:256] = kq[s, 0:B, :]
    rcol, rrow = iota((1, NR), 1), iota((NR, 1), 0)
    rcol_block, rrow_block = block_of(rcol, 9), block_of(rrow, 9)
    rcol_off, rrow_off = rcol - B * rcol_block, rrow - B * rrow_block
    source_row = iota((256, NR), 0)
    diag_tile = ones(jnp.logical_or(source_row == rcol_off, source_row == rcol_off + 128 + 2 * B))
    link_tile = ones(iota((128, NR), 0) == rcol_off + B)
    link_turn = ones(iota((NR, 128), 1) == rrow_off + B)
    diag = exact(qq[...], diag_tile)
    above = exact(qq[:, 0:128], link_tile)
    below = exact(qq[:, 0:128], link_turn, ((1,), (1,)), True)
    rotor_plan, stator_plan = plan(scalar_bounds(False), REDUCED_STEPS), plan(scalar_bounds(True), REDUCED_STEPS)
    mid, half_inv, first, scale = (
        jnp.where(stator, jnp.asarray(b, F32), jnp.asarray(a, F32))
        for a, b in zip(
            (rotor_plan[0], 1.0 / rotor_plan[1], rotor_plan[2], rotor_plan[3]),
            (stator_plan[0], 1.0 / stator_plan[1], stator_plan[2], stator_plan[3]),
        )
    )
    same = iota((NR, NR), 0) == iota((NR, NR), 1)
    live = jnp.logical_and(rrow_block < CHAIN, rcol_block < CHAIN)
    red = jnp.where(rcol_block == rrow_block, diag, 0.0)
    red -= jnp.where(rcol_block == rrow_block + 1, above, 0.0)
    red -= jnp.where(rcol_block + 1 == rrow_block, below, 0.0)
    first_scale = jnp.where(stator, jnp.asarray(FIRST_SCALE, F32), jnp.asarray(1.0, F32))
    row_scale, col_scale = (jnp.where(i < B, first_scale, 1.0) for i in (rrow, rcol))
    red = jnp.where(live, red * (row_scale * col_scale), jnp.where(same, mid, 0.0))
    rmat[...] = red
    tred[...] = jnp.where(same, mid - red, -red) * half_inv
    chebyshev(NR, first, half_inv, lhs, rhs, yred, tred, REDUCED_STEPS, False)
    xr = yred[...] * scale
    want = jnp.logical_and(
        jnp.logical_and(iota((128, NR), 1) == iota((128, NR), 0) + B * l, iota((128, NR), 0) < 2 * B),
        iota((128, NR), 1) < B * CHAIN,
    )
    wanted = jnp.where(want, col_scale, 0.0)
    yred[...] = xr
    few = wanted[0:80]
    y = dot3(split(few), split(yred[...]))
    y += dot((few - dot3(split(y), split(rmat[...]))).astype(BF16), yred[...].astype(BF16))
    y += dot((few - dot(y, rmat[...], HIGHEST)).astype(BF16), yred[...].astype(BF16))
    yt_h[80:128], yt_l[80:128] = jnp.zeros((48, NR), BF16), jnp.zeros((48, NR), BF16)
    yt_h[0:80], yt_l[0:80] = split(y * col_scale)

    finish(0)

    place_edges(1)
    send_edges(1)
    sides(1)
    edges(1)
    interface(1)
    add_edges()
    finish(1)
    out_ref[pl.ds(0, B, stride=CELLS), :] = f_ref[NI : NI + B, :]
    for m in range(7):
        out_ref[pl.ds(m + 1, B, stride=CELLS), :] = f_ref[B * m : B * m + B, :]

    for t in range(2):
        for copy in list(edge_copies(t)) + end_copies(t, *ends_of) + end_copies(t, *corrections):
            copy.wait_send()
    for copy in kq_copies():
        copy.wait_send()

    @pl.when(outlet)
    def _():
        for t in range(2):
            for copy in f63_copies(t) + late_copies(t):
                copy.wait_send()
        c63_copy(p + 1).wait_send()

    @pl.when(inlet)
    def _():
        for t in range(2):
            pass_copy(t).wait_send()
            f64_copy(t).wait_send()
            for copy in late_copies(t):
                copy.wait_send()


def body(pitches, field, source, couple, shift, gain, row_map, slide):
    zs = pitches // 2
    vmem = pl.BlockSpec(memory_space=pltpu.VMEM)
    dma = pltpu.SemaphoreType.DMA
    V = pltpu.VMEM
    shapes = [(B * CELLS, LINES), (B * CELLS, LINES), (B * CELLS, B), (CELLS, B), (CELLS, B)]
    shapes = [V(s, F32) for s in shapes] + [V((pitches, LINES), I32), V((1, INST), I32)]
    out = pl.pallas_call(
        functools.partial(kernel, pitches),
        out_shape=jax.ShapeDtypeStruct((B * CELLS, LINES), F32),
        in_specs=[pl.BlockSpec(memory_space=pltpu.HBM)] * 7,
        out_specs=vmem,
        scratch_shapes=shapes + [
            V((NF, LINES), F32), V((NF, LINES), F32), V((NF, LINES), F32),
            V((NI, LINES), F32), V((NI, LINES), F32),
            V((NI, B), F32), V((NI, B), F32),
            V((NI, NI), F32), V((NI, NI), F32), V((NI, NI), F32),
            V((4 * NR, NR), BF16), V((2 * NR, NR), BF16),
            V((NF, NI), BF16), V((NF, NI), BF16),
            V((NI, 128), BF16), V((NI, 128), BF16),
            V((128, 128), F32),
            V((NR, NR), F32), V((NR, NR), F32), V((NR, NR), F32),
            V((128, NR), BF16), V((128, NR), BF16),
            V((NR, 256), F32),
            V((NR, LINES), F32), V((B * (CHAIN + 1) + 5, LINES), F32),
            V((2, INST, LINES, LINES), BF16),
            V((INST, zs, 8, LINES), F32),
            V((2, 8, NF), F32), V((2, 2, 8, NF), F32),
            V((CHAIN, 40, 128), F32),
            V((2, CHAIN, 72, LINES), F32), V((2, CHAIN, 8, 128), F32),
            V((2, B, LINES), F32), V((2, B, LINES), F32),
            V((2, zs, B, LINES), F32), V((2, B, LINES), F32),
            V((2, B, LINES), F32), V((2, B, LINES), F32),
            V((B, B), F32), V((B, B), F32), V((2, B, LINES), F32),
            dma((CHAIN,)), dma((CHAIN,)), dma((2, CHAIN)), dma((2, CHAIN)), dma((2, CHAIN)), dma((2, CHAIN)),
            dma((2, 2)), dma((2, 2)), dma((2, zs)), dma((2, zs)),
            dma((2,)), dma((2,)), dma((2,)), dma((2,)), dma, dma,
            dma((2, CHAIN)), dma((2,)), dma((7,)),
        ],
        compiler_params=pltpu.CompilerParams(
            collective_id=0, has_side_effects=True, vmem_limit_bytes=48 * 2**20
        ),
        name="sweeps",
    )(
        *(pltpu.with_memory_space_constraint(x, pltpu.HBM) for x in (
            field.transpose(1, 0, 2).reshape(B * CELLS, LINES),
            source.transpose(1, 0, 2).reshape(B * CELLS, LINES),
            couple.transpose(1, 0, 2).reshape(B * CELLS, B),
            shift, gain, row_map.reshape(pitches, LINES), slide.reshape(1, INST),
        ))
    )
    return out.reshape(B, CELLS, LINES).transpose(1, 0, 2)


def solution(mesh):
    return jax.shard_map(
        functools.partial(body, mesh.shape["pitch"]),
        mesh=mesh,
        in_specs=(
            P("axial", None, "pitch"),
            P("axial", None, "pitch"),
            P("axial", None, None),
            P("axial", None),
            P("axial", None),
            P(),
            P(),
        ),
        out_specs=P("axial", None, "pitch"),
        check_vma=False,
    )
```
